32 devices in a mesh: rep: 2 (over y), lat: 4 (over z), ch: 2 (over x), sub: 2 (over core).
Axes of the slice: x: 2, y: 2, z: 4, core: 2. Of those that a mesh axis runs over, the one named last changes fastest.
Arguments:
- field: float32 [224, 128, 1440], P(('rep', 'lat'), 'ch'), parts along dimension 0, may hold values from -6 to 6
- legendre: bfloat16 [192, 112, 384], P('sub', 'lat'), as said below
- ownership: int32 [192], replicated, may hold values from 0 to 191, as said below
- w_real: bfloat16 [128, 128], P('ch'), may hold values from -0.375 to 0.375
- w_imag: bfloat16 [128, 128], P('ch'), may hold values from -0.375 to 0.375
Outputs:
- mixed: bfloat16 [4, 192, 128, 384], P('rep', ('lat', 'sub'), 'ch'), parts along dimension 0
The draws below stay inside these ranges and needn't reach their ends.
There are 2 independent parts, one for each index of `rep`. The reference program is written for one: setup_inputs(seed, part) draws one part's arguments, and reference() takes and returns one part's arrays. A program takes and returns all parts, laid end to end along the dimension named above; an argument that names none is the same for every part. Nothing has to cross between parts.
Inputs may be any that keep to these rules, and one draw needn't show every extreme that they name: `ownership`: A permutation of 0 to 191. With S the number of devices of sub, the positions p with (p // 24) % S = s hold the wavenumbers s * 192 / S to (s + 1) * 192 / S - 1, and entries 2i and 2i + 1 are some m of that range and the wavenumber as far from the range's other end. `legendre`: zero wherever the degree l is below the wavenumber m.
All inputs are finite; a program needn't handle non-finite values.
Results may differ from the reference program's by a relative error of at most 0.014.
Values may be sent and summed in bfloat16 or wider, within the bound.
No kernel may reach another device: no remote copies, remote signals or barrier semaphores. Data moves between devices by JAX's collectives and lax.ppermute only.
A program may use at most 128 MiB of HBM per device.

```python
import math
import jax
import jax.numpy as jnp
from jax import lax

C = 128
NLON = 1440
L = 384
MM = 192
LAT_DEV = 28
NLAT = 112
K = 24
N_LAT = 4
N_SUB = 2


def draw_legendre(key, part):
    key = jax.random.fold_in(key, 11)
    degree = jnp.arange(L)[None, None, :]
    wavenumber = jnp.arange(MM)[:, None, None]
    values = jnp.clip(jax.random.normal(key, (MM, NLAT, L), jnp.float32), -4.0, 4.0)
    keep = (degree >= wavenumber).astype(jnp.float32)
    return (values * keep / jnp.sqrt(jnp.float32(NLAT))).astype(jnp.bfloat16)


def draw_ownership(key, part):
    key = jax.random.fold_in(key, 17)
    share = MM // N_SUB
    lists = []
    for index in range(N_SUB):
        lower = jax.random.permutation(jax.random.fold_in(key, index), share // 2).astype(jnp.int32)
        paired = jnp.stack([index * share + lower, index * share + share - 1 - lower], axis=1)
        lists.append(paired.reshape(N_LAT, K))
    return jnp.stack(lists, axis=1).reshape(MM).astype(jnp.int32)


def levels(rng, dims, shards, smallest, largest):
    def one(position, shards_of):
        draws = jax.random.uniform(jax.random.fold_in(jax.random.fold_in(rng, 6), position), (shards_of,), jnp.float32, smallest / len(shards), largest / len(shards))
        return jnp.repeat(jnp.exp(draws), dims[position] // shards_of).reshape((-1,) + (1,) * (len(dims) - position - 1))

    factor_of = one(*shards[0])
    for cut in shards[1:]:
        factor_of = factor_of * one(*cut)
    return factor_of


def normal_values(stream_key, dims, width, bound, split=(), kind=jnp.bfloat16):
    gain = levels(stream_key, dims, split, -0.22, 0.18) if split else 1.0
    values = jax.random.normal(stream_key, dims, jnp.float32) * width * gain
    return jnp.minimum(jnp.maximum(values, -bound), bound).astype(kind)


def setup_inputs(seed: int = 0, part: int = 0) -> dict:
    streams_of = jax.random.split(jax.random.key(seed), 6)
    own_keys = jax.random.split(jax.random.fold_in(streams_of[5], part), 6)
    return {
        "field": normal_values(own_keys[0], (NLAT, C, NLON), 1.0, 6.0, ((0, 4), (1, 2)), jnp.float32),
        "legendre": draw_legendre(jax.random.fold_in(streams_of[5], 71), part),
        "ownership": draw_ownership(jax.random.fold_in(streams_of[5], 71), part),
        "w_real": normal_values(streams_of[3], (C, C), (2 * C) ** -0.5, 0.375, ((0, 2),)),
        "w_imag": normal_values(streams_of[4], (C, C), (2 * C) ** -0.5, 0.375, ((0, 2),)),
    }


def reference(field, legendre, ownership, w_real, w_imag):
    spectrum = jnp.fft.rfft(field, axis=-1)[..., :MM] / math.sqrt(NLON)
    fourier = jnp.stack([jnp.real(spectrum), jnp.imag(spectrum)]).astype(jnp.bfloat16)
    per_mode = jnp.moveaxis(fourier, 3, 0)

    def one_mode(pair):
        values, table = pair
        values = values.astype(jnp.float32).reshape(2, N_LAT, LAT_DEV, C)
        table = table.astype(jnp.float32).reshape(N_LAT, LAT_DEV, L)
        block = jnp.einsum('rbtc,btl->rbcl', values, table).astype(jnp.bfloat16)
        return lax.optimization_barrier(jnp.sum(block.astype(jnp.float32), axis=1)).astype(jnp.bfloat16)
    coeff = lax.map(one_mode, (per_mode, legendre))
    owned = jnp.take(coeff, ownership.astype(jnp.int32), axis=0).astype(jnp.float32)
    real_w = w_real.astype(jnp.float32)
    imag_w = w_imag.astype(jnp.float32)
    real_out = jnp.einsum('oc,pcl->pol', real_w, owned[:, 0]) - jnp.einsum('oc,pcl->pol', imag_w, owned[:, 1])
    imag_out = jnp.einsum('oc,pcl->pol', real_w, owned[:, 1]) + jnp.einsum('oc,pcl->pol', imag_w, owned[:, 0])
    return jnp.stack([real_out, imag_out]).astype(jnp.bfloat16)
```

```python
import functools
import math

import jax
import jax.numpy as jnp
import numpy as np
from jax import lax
from jax.experimental import pallas as pl
from jax.experimental.pallas import tpu as pltpu
from jax.sharding import PartitionSpec as P

F32 = jnp.float32
BF16 = jnp.bfloat16


def twiddles(nlon, modes):
    phase = np.arange(nlon)[:, None] * np.arange(modes)[None, :] % nlon
    angle = phase * (2.0 * math.pi / nlon)
    scale = 1.0 / math.sqrt(nlon)
    return np.stack([np.cos(angle) * scale, -np.sin(angle) * scale]).astype(BF16)


def position(shift, k, sizes):
    owner = lax.rem(lax.axis_index("lat") + shift, sizes["lat"])
    return (owner * sizes["sub"] + lax.axis_index("sub")) * sizes["per"] + k


def owned_row(owner_ref, sizes, shifts):
    lane = lax.broadcasted_iota(jnp.int32, (1, 128), 1)
    row = jnp.full((1, 128), -1, jnp.int32)
    j = 0
    for shift in shifts:
        base = position(shift, 0, sizes)
        for k in range(sizes["per"]):
            row = jnp.where(lane == j, owner_ref[base + k], row)
            j += 1
    return row


def dft_kernel(sizes, owner_ref, table_ref, field_ref, *refs):
    outs, chosen = refs[:-1], refs[-1]
    per = sizes["per"]

    @pl.when(pl.program_id(0) == 0)
    def _():
        row = owned_row(owner_ref, sizes, range(sizes["lat"]))
        modes = table_ref.shape[2]
        pick = (lax.broadcasted_iota(jnp.int32, (modes, 128), 0) == row).astype(F32).astype(BF16)
        for r in range(2):
            chosen[:, r * 128 : (r + 1) * 128] = jnp.dot(
                table_ref[r], pick, preferred_element_type=F32
            ).astype(BF16)

    rows, chans, nlon = field_ref.shape
    grid_values = field_ref[...].reshape(rows * chans, nlon).astype(BF16)
    spectrum = jnp.dot(grid_values, chosen[...], preferred_element_type=F32)
    for t in range(rows):
        part = spectrum[t * chans : (t + 1) * chans]
        both = jnp.concatenate([part[:, :128], part[:, 128:]], axis=0)
        turned = both.T
        for shift in range(sizes["lat"]):
            outs[shift][t] = turned[shift * per : (shift + 1) * per].astype(BF16)


def dft(field, ownership, sizes):
    lat_rows, chans, nlon = field.shape
    modes = ownership.shape[0]
    step = 4
    per = sizes["per"]
    table = jnp.asarray(twiddles(nlon, modes))
    return pl.pallas_call(
        functools.partial(dft_kernel, sizes),
        grid=(lat_rows // step,),
        in_specs=[
            pl.BlockSpec(memory_space=pltpu.SMEM),
            pl.BlockSpec((2, nlon, modes), lambda i: (0, 0, 0)),
            pl.BlockSpec((step, chans, nlon), lambda i: (i, 0, 0)),
        ],
        out_specs=[pl.BlockSpec((step, per, 128), lambda i: (i, 0, 0))] * sizes["lat"],
        out_shape=[jax.ShapeDtypeStruct((lat_rows, per, 128), BF16)] * sizes["lat"],
        scratch_shapes=[pltpu.VMEM((nlon, 256), BF16)],
        compiler_params=pltpu.CompilerParams(vmem_limit_bytes=40 << 20),
        cost_estimate=pl.CostEstimate(
            flops=2 * lat_rows * chans * nlon * 256, bytes_accessed=field.size * 4, transcendentals=0
        ),
        name="dft",
    )(ownership, table, field)


def pick_kernel(sizes, shifts, owner_ref, legendre_ref, *outs):
    per = sizes["per"]
    row = owned_row(owner_ref, sizes, shifts) - lax.axis_index("sub") * legendre_ref.shape[1]
    pick = (lax.broadcasted_iota(jnp.int32, (legendre_ref.shape[1], 128), 0) == row).astype(F32)
    pick = pick.T[: len(shifts) * per].astype(BF16)
    for t in range(legendre_ref.shape[0]):
        rows = jnp.dot(pick, legendre_ref[t], preferred_element_type=F32)
        for i in range(len(shifts)):
            outs[i][t] = rows[i * per : (i + 1) * per].astype(BF16)


def pick_rows(table, ownership, sizes, shifts, rows, mine):
    _, slab, degrees = table.shape
    per = sizes["per"]
    share = lambda: lax.axis_index("rep") * sizes["ch"] + lax.axis_index("ch") if mine else 0
    return pl.pallas_call(
        functools.partial(pick_kernel, sizes, shifts),
        grid=(1,),
        in_specs=[
            pl.BlockSpec(memory_space=pltpu.SMEM),
            pl.BlockSpec((rows, slab, degrees), lambda i: (share(), 0, 0)),
        ],
        out_specs=[pl.BlockSpec((rows, per, degrees), lambda i: (0, 0, 0))] * len(shifts),
        out_shape=[jax.ShapeDtypeStruct((rows, per, degrees), BF16)] * len(shifts),
        compiler_params=pltpu.CompilerParams(vmem_limit_bytes=40 << 20),
        cost_estimate=pl.CostEstimate(
            flops=2 * rows * slab * degrees * per * len(shifts),
            bytes_accessed=rows * slab * degrees * 2,
            transcendentals=0,
        ),
        name="pick_rows",
    )(ownership, table)


def contract_kernel(sizes, group, *refs):
    lats, plane, per = sizes["lat"], sizes["rep"] * sizes["ch"], sizes["per"]
    near, refs = refs[:lats], refs[lats:]
    far, refs = refs[:lats], refs[lats:]
    own_table, refs = refs[0], refs[1:]
    tables, refs = refs[: plane * (lats - 1)], refs[plane * (lats - 1) :]
    w_near, w_far, out_ref, spectra, table = refs
    lat_rows = near[0].shape[0]
    share = lat_rows // plane
    depth = lats * lat_rows
    block = share * per

    @pl.when(pl.program_id(0) == 0)
    def _():
        q = lax.axis_index("rep") * sizes["ch"] + lax.axis_index("ch")
        nt = (((1,), (1,)), ((), ()))
        for s in range(lats):
            for d in range(plane):
                first = d * share if s == 0 else jnp.bitwise_xor(q, d) * share
                a = near[s][pl.ds(first, share)].reshape(block, 128)
                b = far[s][pl.ds(first, share)].reshape(block, 128)
                mixed = lax.dot_general(a, w_near[...], nt, preferred_element_type=F32)
                mixed += lax.dot_general(b, w_far[...], nt, preferred_element_type=F32)
                at = (s * plane + d) * block
                spectra[at : at + block, :] = mixed
                if s == 0:
                    values = own_table[d * share : (d + 1) * share]
                else:
                    values = tables[d * (lats - 1) + s - 1][...]
                values = values.astype(F32).reshape(block, values.shape[-1])
                for tile in range(table.shape[0]):
                    table[tile, at : at + block, :] = values[:, tile * 128 : (tile + 1) * 128]

    first = pl.program_id(0) * group
    half = out_ref.shape[2]
    for k in range(group):
        a = spectra[pl.ds(first + k, depth, stride=per), :].astype(BF16)
        b = jnp.concatenate(
            [table[i, pl.ds(first + k, depth, stride=per), :] for i in range(table.shape[0])], axis=1
        ).astype(BF16)
        c = lax.dot_general(a, b, (((0,), (0,)), ((), ())), preferred_element_type=F32)
        out_ref[0, k] = c[:half].astype(BF16)
        out_ref[1, k] = c[half:].astype(BF16)


def contract(near, far, own_table, tables, w_near, w_far, sizes):
    lat_rows, per, _ = near[0].shape
    degrees = own_table.shape[2]
    half = w_near.shape[0] // 2
    group = 8
    depth = sizes["lat"] * lat_rows
    operands = [*near, *far, own_table, *tables, w_near, w_far]
    whole = lambda x: pl.BlockSpec(x.shape, lambda i: (0,) * x.ndim)
    return pl.pallas_call(
        functools.partial(contract_kernel, sizes, group),
        grid=(per // group,),
        in_specs=[whole(x) for x in operands],
        out_specs=pl.BlockSpec((2, group, half, degrees), lambda i: (0, i, 0, 0)),
        out_shape=jax.ShapeDtypeStruct((2, per, half, degrees), BF16),
        scratch_shapes=[pltpu.VMEM((depth * per, 128), F32), pltpu.VMEM((degrees // 128, depth * per, 128), F32)],
        compiler_params=pltpu.CompilerParams(vmem_limit_bytes=48 << 20),
        name="contract",
    )(*operands)


def mixing_weights(w_real, w_imag):
    half = w_real.shape[0]
    x = lax.axis_index("ch")
    out = []
    for side in (x, 1 - x):
        wr = lax.dynamic_slice_in_dim(w_real, side * half, half, 1)
        wi = lax.dynamic_slice_in_dim(w_imag, side * half, half, 1)
        out.append(
            jnp.concatenate(
                [jnp.concatenate([wr, -wi], axis=1), jnp.concatenate([wi, wr], axis=1)], axis=0
            )
        )
    return out


def fast(field, legendre, ownership, w_real, w_imag, sizes):
    lats, plane = sizes["lat"], sizes["rep"] * sizes["ch"]
    lat_rows = field.shape[0]
    by_latitude = jnp.transpose(legendre, (1, 0, 2))
    turn = lambda s: [(i, (i + s) % lats) for i in range(lats)]
    flip = lambda d: [(i, i ^ d) for i in range(plane)]
    others = tuple(range(1, lats))
    sent = pick_rows(by_latitude, ownership, sizes, others, lat_rows // plane, True)
    landed = [lax.ppermute(sent[s - 1], "lat", turn(s)) for s in others]
    spectra = dft(field, ownership, sizes)
    near = [spectra[0]] + [lax.ppermute(spectra[s], "lat", turn(s)) for s in others]
    far = [lax.ppermute(v, "ch", [(0, 1), (1, 0)]) for v in near]
    tables = list(landed)
    for d in range(1, plane):
        tables += [lax.ppermute(v, ("rep", "ch"), flip(d)) for v in landed]
    (own_table,) = pick_rows(by_latitude, ownership, sizes, (0,), lat_rows, False)
    w_near, w_far = mixing_weights(w_real, w_imag)
    return contract(near, far, own_table, tables, w_near, w_far, sizes)


def fourier_rows(flat_field, modes, lat_rows, chans, nlon):
    longitude = jnp.arange(nlon, dtype=jnp.int32)
    phase = longitude[:, None] * modes[None, :] % nlon
    angle = phase.astype(jnp.float32) * (2.0 * math.pi / nlon)
    scale = 1.0 / math.sqrt(nlon)
    real_part = (
        jnp.dot(
            flat_field,
            jnp.cos(angle),
            precision=lax.Precision.HIGHEST,
            preferred_element_type=jnp.float32,
        )
        * scale
    )
    imag_part = (
        -jnp.dot(
            flat_field,
            jnp.sin(angle),
            precision=lax.Precision.HIGHEST,
            preferred_element_type=jnp.float32,
        )
        * scale
    )
    both = jnp.stack([real_part, imag_part]).reshape(2, lat_rows, chans, modes.shape[0])
    both = jnp.transpose(both, (3, 1, 0, 2)).reshape(modes.shape[0], lat_rows, 2 * chans)
    return both.astype(jnp.bfloat16)


def general(field, legendre, ownership, w_real, w_imag):
    lat_rows, chans, nlon = field.shape
    degrees = legendre.shape[2]
    slab_modes = legendre.shape[0]
    blocks = lax.axis_size("lat")
    halves = lax.axis_size("sub")
    per_block = ownership.shape[0] // (blocks * halves)
    my_modes = lax.dynamic_index_in_dim(
        ownership.reshape(blocks, halves, per_block), lax.axis_index("sub"), 1, keepdims=False
    ).reshape(blocks * per_block)
    slab_index = my_modes - lax.axis_index("sub") * slab_modes
    flat_field = field.reshape(lat_rows * chans, nlon)
    spectra_rows = fourier_rows(flat_field, my_modes, lat_rows, chans, nlon)
    table_rows = jnp.take(legendre, slab_index, axis=0)
    spectra_all, tables_all = (
        lax.all_to_all(spectra_rows, "lat", split_axis=0, concat_axis=1, tiled=True),
        lax.all_to_all(table_rows, "lat", split_axis=0, concat_axis=1, tiled=True),
    )
    spectra_all = spectra_all.reshape(per_block, blocks, lat_rows, 2 * chans)
    tables_all = tables_all.reshape(per_block, blocks, lat_rows, degrees)
    block_part = jnp.einsum(
        "kbtc,kbtl->kbcl", spectra_all, tables_all, preferred_element_type=jnp.float32
    )
    total = jnp.sum(block_part, axis=1)
    coeff = total.astype(jnp.bfloat16).reshape(per_block, 2, chans, degrees)
    piece = lax.all_gather(coeff, "ch", axis=2, tiled=True)
    real_in = piece[:, 0]
    imag_in = piece[:, 1]
    real_out = jnp.einsum(
        "oc,kcl->kol", w_real, real_in, preferred_element_type=jnp.float32
    ) - jnp.einsum("oc,kcl->kol", w_imag, imag_in, preferred_element_type=jnp.float32)
    imag_out = jnp.einsum(
        "oc,kcl->kol", w_real, imag_in, preferred_element_type=jnp.float32
    ) + jnp.einsum("oc,kcl->kol", w_imag, real_in, preferred_element_type=jnp.float32)
    mixed = jnp.stack([real_out, imag_out])
    return mixed.astype(jnp.bfloat16)


def per_device(sizes, field, legendre, ownership, w_real, w_imag):
    lat_rows, chans, nlon = field.shape
    sizes = dict(sizes, per=ownership.shape[0] // (sizes["lat"] * sizes["sub"]))
    plane = sizes["rep"] * sizes["ch"]
    fits = (
        sizes["ch"] == 2
        and 2 * chans == 128
        and plane & (plane - 1) == 0
        and lat_rows % plane == 0
        and lat_rows % 4 == 0
        and sizes["per"] % 8 == 0
        and sizes["lat"] * sizes["per"] <= 128
        and legendre.shape[2] % 128 == 0
    )
    if fits:
        return fast(field, legendre, ownership, w_real, w_imag, sizes)
    return general(field, legendre, ownership, w_real, w_imag)


def solution(mesh):
    in_specs = (
        P(("rep", "lat"), "ch", None),
        P("sub", "lat", None),
        P(),
        P("ch", None),
        P("ch", None),
    )
    out_specs = P("rep", ("lat", "sub"), "ch", None)
    return jax.shard_map(
        functools.partial(per_device, dict(mesh.shape)),
        mesh=mesh,
        in_specs=in_specs,
        out_specs=out_specs,
        check_vma=False,
    )
```

```python
import functools
import math

import jax
import jax.numpy as jnp
import numpy as np
from jax import lax
from jax.experimental import pallas as pl
from jax.experimental.pallas import tpu as pltpu
from jax.sharding import PartitionSpec as P

F32 = jnp.float32
BF16 = jnp.bfloat16


def twiddles(nlon, modes):
    phase = np.arange(nlon)[:, None] * np.arange(modes)[None, :] % nlon
    angle = phase * (2.0 * math.pi / nlon)
    scale = 1.0 / math.sqrt(nlon)
    return np.stack([np.cos(angle) * scale, -np.sin(angle) * scale]).astype(BF16)


def position(shift, k, sizes):
    owner = lax.rem(lax.axis_index("lat") + shift, sizes["lat"])
    return (owner * sizes["sub"] + lax.axis_index("sub")) * sizes["per"] + k


def owned_row(owner_ref, sizes, shifts):
    lane = lax.broadcasted_iota(jnp.int32, (1, 128), 1)
    row = jnp.full((1, 128), -1, jnp.int32)
    j = 0
    for shift in shifts:
        base = position(shift, 0, sizes)
        for k in range(sizes["per"]):
            row = jnp.where(lane == j, owner_ref[base + k], row)
            j += 1
    return row


def dft_kernel(sizes, step, owner_ref, table_ref, field_ref, *refs):
    *outs, grid_values, chosen, arrived = refs
    per = sizes["per"]
    rows, chans, nlon = grid_values.shape

    def part_copy(i):
        part = pl.ds(i * step, step)
        return pltpu.make_async_copy(field_ref.at[part], grid_values.at[part], arrived.at[i])

    for i in range(rows // step):
        part_copy(i).start()

    row = owned_row(owner_ref, sizes, range(sizes["lat"]))
    modes = table_ref.shape[2]
    pick = (lax.broadcasted_iota(jnp.int32, (modes, 128), 0) == row).astype(F32).astype(BF16)
    for r in range(2):
        chosen[:, r * 128 : (r + 1) * 128] = jnp.dot(
            table_ref[r], pick, preferred_element_type=F32
        ).astype(BF16)

    @pl.loop(0, rows // step)
    def _(i):
        part_copy(i).wait()
        values = grid_values[pl.ds(i * step, step)].reshape(step * chans, nlon).astype(BF16)
        spectrum = jnp.dot(values, chosen[...], preferred_element_type=F32)
        for t in range(step):
            part = spectrum[t * chans : (t + 1) * chans]
            turned = jnp.concatenate([part[:, :128], part[:, 128:]], axis=0).T
            for shift in range(sizes["lat"]):
                outs[shift][i * step + t] = turned[shift * per : (shift + 1) * per].astype(BF16)


def dft(field, ownership, sizes):
    lat_rows, chans, nlon = field.shape
    modes = ownership.shape[0]
    step = 4
    per = sizes["per"]
    table = jnp.asarray(twiddles(nlon, modes))
    vmem = pl.BlockSpec(memory_space=pltpu.VMEM)
    return pl.pallas_call(
        functools.partial(dft_kernel, sizes, step),
        in_specs=[
            pl.BlockSpec(memory_space=pltpu.SMEM),
            vmem,
            pl.BlockSpec(memory_space=pl.ANY),
        ],
        out_specs=[vmem] * sizes["lat"],
        out_shape=[jax.ShapeDtypeStruct((lat_rows, per, 128), BF16)] * sizes["lat"],
        scratch_shapes=[
            pltpu.VMEM(field.shape, F32),
            pltpu.VMEM((nlon, 256), BF16),
            pltpu.SemaphoreType.DMA((lat_rows // step,)),
        ],
        compiler_params=pltpu.CompilerParams(vmem_limit_bytes=52 << 20),
        cost_estimate=pl.CostEstimate(
            flops=2 * lat_rows * chans * nlon * 256, bytes_accessed=field.size * 4, transcendentals=0
        ),
        name="dft",
    )(ownership, table, field)


def pick_kernel(sizes, shifts, owner_ref, legendre_ref, *outs):
    per = sizes["per"]
    row = owned_row(owner_ref, sizes, shifts) - lax.axis_index("sub") * legendre_ref.shape[1]
    pick = (lax.broadcasted_iota(jnp.int32, (legendre_ref.shape[1], 128), 0) == row).astype(F32)
    pick = pick.T[: len(shifts) * per].astype(BF16)
    for t in range(legendre_ref.shape[0]):
        rows = jnp.dot(pick, legendre_ref[t], preferred_element_type=F32)
        for i in range(len(shifts)):
            outs[i][t] = rows[i * per : (i + 1) * per].astype(BF16)


def pick_rows(table, ownership, sizes, shifts, rows):
    _, slab, degrees = table.shape
    per = sizes["per"]
    return pl.pallas_call(
        functools.partial(pick_kernel, sizes, shifts),
        grid=(1,),
        in_specs=[
            pl.BlockSpec(memory_space=pltpu.SMEM),
            pl.BlockSpec(
                (rows, slab, degrees),
                lambda i: (lax.axis_index("rep") * sizes["ch"] + lax.axis_index("ch"), 0, 0),
            ),
        ],
        out_specs=[pl.BlockSpec((rows, per, degrees), lambda i: (0, 0, 0))] * len(shifts),
        out_shape=[jax.ShapeDtypeStruct((rows, per, degrees), BF16)] * len(shifts),
        compiler_params=pltpu.CompilerParams(vmem_limit_bytes=60 << 20),
        cost_estimate=pl.CostEstimate(
            flops=2 * rows * slab * degrees * per * len(shifts),
            bytes_accessed=rows * slab * degrees * 2,
            transcendentals=0,
        ),
        name="pick_rows",
    )(ownership, table)


def pack_kernel(*refs):
    *parts, out_ref = refs
    share = parts[0].shape[0]
    for i, part in enumerate(parts):
        out_ref[i * share : (i + 1) * share] = part[...]


def pack(parts):
    share, per, degrees = parts[0].shape
    return pl.pallas_call(
        pack_kernel,
        out_shape=jax.ShapeDtypeStruct((len(parts) * share, per, degrees), BF16),
        compiler_params=pltpu.CompilerParams(vmem_limit_bytes=16 << 20),
        name="pack",
    )(*parts)


def turn_kernel(sizes, owner_ref, legendre_ref, *refs):
    *shares, out_ref, table = refs
    per, lats, plane = sizes["per"], sizes["lat"], sizes["rep"] * sizes["ch"]
    lat_rows, slab, degrees = legendre_ref.shape
    deep = out_ref.shape[1] // lats
    share = lat_rows // plane
    tiles = degrees // 128
    for s in range(lats):
        end = (s * deep + lat_rows) * per
        table[:, end : (s + 1) * deep * per, :] = jnp.zeros((tiles, (deep - lat_rows) * per, 128), F32)
    row = owned_row(owner_ref, sizes, (0,)) - lax.axis_index("sub") * slab
    pick = (lax.broadcasted_iota(jnp.int32, (slab, 128), 0) == row).astype(F32)
    pick = pick.T[:per].astype(BF16)
    for t in range(lat_rows):
        rows = jnp.dot(pick, legendre_ref[t], preferred_element_type=F32)
        for i in range(tiles):
            table[i, t * per : (t + 1) * per, :] = rows[:, i * 128 : (i + 1) * 128]
    block = share * per
    q = lax.axis_index("rep") * sizes["ch"] + lax.axis_index("ch")
    for s in range(1, lats):
        for d in range(plane):
            values = shares[d][(s - 1) * share : s * share].astype(F32).reshape(block, degrees)
            at = pl.multiple_of((s * deep + jnp.bitwise_xor(q, d) * share) * per, 8)
            for i in range(tiles):
                table[i, pl.ds(at, block), :] = values[:, i * 128 : (i + 1) * 128]
    for k in range(per):
        for i in range(tiles):
            out_ref[k, :, i * 128 : (i + 1) * 128] = table[
                i, pl.ds(k, lats * deep, stride=per), :
            ].astype(BF16)


def turn(by_latitude, ownership, shares, deep, sizes):
    lat_rows, _, degrees = by_latitude.shape
    per, depth = sizes["per"], sizes["lat"] * deep
    vmem = pl.BlockSpec(memory_space=pltpu.VMEM)
    return pl.pallas_call(
        functools.partial(turn_kernel, sizes),
        in_specs=[pl.BlockSpec(memory_space=pltpu.SMEM)] + [vmem] * (1 + len(shares)),
        out_specs=vmem,
        out_shape=jax.ShapeDtypeStruct((per, depth, degrees), BF16),
        scratch_shapes=[pltpu.VMEM((degrees // 128, depth * per, 128), F32)],
        compiler_params=pltpu.CompilerParams(vmem_limit_bytes=32 << 20),
        name="turn",
    )(ownership, by_latitude, *shares)


def mix_kernel(near_ref, far_ref, w_near, w_far, out_ref, spectra):
    lat_rows, per, width = near_ref.shape
    deep = out_ref.shape[1]
    nt = (((1,), (1,)), ((), ()))
    a = near_ref[...].reshape(lat_rows * per, width)
    b = far_ref[...].reshape(lat_rows * per, width)
    mixed = lax.dot_general(a, w_near[...], nt, preferred_element_type=F32)
    mixed += lax.dot_general(b, w_far[...], nt, preferred_element_type=F32)
    spectra[: lat_rows * per, :] = mixed
    spectra[lat_rows * per :, :] = jnp.zeros(((deep - lat_rows) * per, width), F32)
    for k in range(per):
        out_ref[k] = spectra[pl.ds(k, deep, stride=per), :].astype(BF16)


def mix(near, far, w_near, w_far, deep):
    lat_rows, per, width = near.shape
    return pl.pallas_call(
        mix_kernel,
        out_shape=jax.ShapeDtypeStruct((per, deep, width), BF16),
        scratch_shapes=[pltpu.VMEM((deep * per, width), F32)],
        compiler_params=pltpu.CompilerParams(vmem_limit_bytes=16 << 20),
        cost_estimate=pl.CostEstimate(
            flops=100 * 2 * near.size * width, bytes_accessed=near.size * 4, transcendentals=0
        ),
        name="mix",
    )(near, far, w_near, w_far)


def contract_kernel(group, *refs):
    *spectra, table, out_ref = refs
    half = out_ref.shape[2]
    for k in range(group):
        a = jnp.concatenate([part[k] for part in spectra], axis=0)
        c = lax.dot_general(a, table[k], (((0,), (0,)), ((), ())), preferred_element_type=F32)
        out_ref[0, k] = c[:half].astype(BF16)
        out_ref[1, k] = c[half:].astype(BF16)


def contract(spectra, table):
    per, deep, width = spectra[0].shape
    _, depth, degrees = table.shape
    group = 8
    block = lambda x: pl.BlockSpec((group, *x.shape[1:]), lambda i: (i, 0, 0))
    return pl.pallas_call(
        functools.partial(contract_kernel, group),
        grid=(per // group,),
        in_specs=[block(x) for x in (*spectra, table)],
        out_specs=pl.BlockSpec((2, group, width // 2, degrees), lambda i: (0, i, 0, 0)),
        out_shape=jax.ShapeDtypeStruct((2, per, width // 2, degrees), BF16),
        compiler_params=pltpu.CompilerParams(vmem_limit_bytes=40 << 20),
        name="contract",
    )(*spectra, table)


def mixing_weights(w_real, w_imag):
    half = w_real.shape[0]
    x = lax.axis_index("ch")
    out = []
    for side in (x, 1 - x):
        wr = lax.dynamic_slice_in_dim(w_real, side * half, half, 1)
        wi = lax.dynamic_slice_in_dim(w_imag, side * half, half, 1)
        out.append(
            jnp.concatenate(
                [jnp.concatenate([wr, -wi], axis=1), jnp.concatenate([wi, wr], axis=1)], axis=0
            )
        )
    return out


def fast(field, legendre, ownership, w_real, w_imag, sizes):
    lats, plane = sizes["lat"], sizes["rep"] * sizes["ch"]
    lat_rows = field.shape[0]
    by_latitude = jnp.transpose(legendre, (1, 0, 2))
    along = lambda s: [(i, (i + s) % lats) for i in range(lats)]
    swap = [(0, 1), (1, 0)]
    others = tuple(range(1, lats))
    sent = pick_rows(by_latitude, ownership, sizes, others, lat_rows // plane)
    landed = [lax.ppermute(sent[s - 1], "lat", along(s)) for s in others]
    after_sent, _ = lax.optimization_barrier((ownership, sent[0]))
    spectra = dft(field, after_sent, sizes)
    landed, starts = lax.optimization_barrier((landed, spectra[1:]))
    near = [spectra[0]] + [lax.ppermute(v, "lat", along(s)) for s, v in zip(others, starts)]
    far = [lax.ppermute(v, "ch", swap) for v in near]
    mine = pack(landed)
    beside = lax.ppermute(mine, "ch", swap)
    shares = [mine, beside, lax.ppermute(mine, "rep", swap), lax.ppermute(beside, "rep", swap)]
    deep = (lat_rows + 15) // 16 * 16
    table = turn(by_latitude, ownership, shares, deep, sizes)
    w_near, w_far = mixing_weights(w_real, w_imag)
    mixed = [mix(n, f, w_near, w_far, deep) for n, f in zip(near, far)]
    return contract(mixed, table)


def fourier_rows(flat_field, modes, lat_rows, chans, nlon):
    longitude = jnp.arange(nlon, dtype=jnp.int32)
    phase = longitude[:, None] * modes[None, :] % nlon
    angle = phase.astype(jnp.float32) * (2.0 * math.pi / nlon)
    scale = 1.0 / math.sqrt(nlon)
    real_part = (
        jnp.dot(
            flat_field,
            jnp.cos(angle),
            precision=lax.Precision.HIGHEST,
            preferred_element_type=jnp.float32,
        )
        * scale
    )
    imag_part = (
        -jnp.dot(
            flat_field,
            jnp.sin(angle),
            precision=lax.Precision.HIGHEST,
            preferred_element_type=jnp.float32,
        )
        * scale
    )
    both = jnp.stack([real_part, imag_part]).reshape(2, lat_rows, chans, modes.shape[0])
    both = jnp.transpose(both, (3, 1, 0, 2)).reshape(modes.shape[0], lat_rows, 2 * chans)
    return both.astype(jnp.bfloat16)


def general(field, legendre, ownership, w_real, w_imag):
    lat_rows, chans, nlon = field.shape
    degrees = legendre.shape[2]
    slab_modes = legendre.shape[0]
    blocks = lax.axis_size("lat")
    halves = lax.axis_size("sub")
    per_block = ownership.shape[0] // (blocks * halves)
    my_modes = lax.dynamic_index_in_dim(
        ownership.reshape(blocks, halves, per_block), lax.axis_index("sub"), 1, keepdims=False
    ).reshape(blocks * per_block)
    slab_index = my_modes - lax.axis_index("sub") * slab_modes
    flat_field = field.reshape(lat_rows * chans, nlon)
    spectra_rows = fourier_rows(flat_field, my_modes, lat_rows, chans, nlon)
    table_rows = jnp.take(legendre, slab_index, axis=0)
    spectra_all, tables_all = (
        lax.all_to_all(spectra_rows, "lat", split_axis=0, concat_axis=1, tiled=True),
        lax.all_to_all(table_rows, "lat", split_axis=0, concat_axis=1, tiled=True),
    )
    spectra_all = spectra_all.reshape(per_block, blocks, lat_rows, 2 * chans)
    tables_all = tables_all.reshape(per_block, blocks, lat_rows, degrees)
    block_part = jnp.einsum(
        "kbtc,kbtl->kbcl", spectra_all, tables_all, preferred_element_type=jnp.float32
    )
    total = jnp.sum(block_part, axis=1)
    coeff = total.astype(jnp.bfloat16).reshape(per_block, 2, chans, degrees)
    piece = lax.all_gather(coeff, "ch", axis=2, tiled=True)
    real_in = piece[:, 0]
    imag_in = piece[:, 1]
    real_out = jnp.einsum(
        "oc,kcl->kol", w_real, real_in, preferred_element_type=jnp.float32
    ) - jnp.einsum("oc,kcl->kol", w_imag, imag_in, preferred_element_type=jnp.float32)
    imag_out = jnp.einsum(
        "oc,kcl->kol", w_real, imag_in, preferred_element_type=jnp.float32
    ) + jnp.einsum("oc,kcl->kol", w_imag, real_in, preferred_element_type=jnp.float32)
    mixed = jnp.stack([real_out, imag_out])
    return mixed.astype(jnp.bfloat16)


def per_device(sizes, field, legendre, ownership, w_real, w_imag):
    lat_rows, chans, nlon = field.shape
    sizes = dict(sizes, per=ownership.shape[0] // (sizes["lat"] * sizes["sub"]))
    plane = sizes["rep"] * sizes["ch"]
    fits = (
        sizes["ch"] == 2
        and sizes["rep"] == 2
        and 2 * chans == 128
        and lat_rows % plane == 0
        and lat_rows % 4 == 0
        and sizes["per"] % 8 == 0
        and sizes["lat"] * sizes["per"] <= 128
        and legendre.shape[2] % 128 == 0
    )
    if fits:
        return fast(field, legendre, ownership, w_real, w_imag, sizes)
    return general(field, legendre, ownership, w_real, w_imag)


def solution(mesh):
    in_specs = (
        P(("rep", "lat"), "ch", None),
        P("sub", "lat", None),
        P(),
        P("ch", None),
        P("ch", None),
    )
    out_specs = P("rep", ("lat", "sub"), "ch", None)
    return jax.shard_map(
        functools.partial(per_device, dict(mesh.shape)),
        mesh=mesh,
        in_specs=in_specs,
        out_specs=out_specs,
        check_vma=False,
    )
```

```python
import functools
import math

import jax
import jax.numpy as jnp
import numpy as np
from jax import lax
from jax.experimental import pallas as pl
from jax.experimental.pallas import tpu as pltpu
from jax.sharding import PartitionSpec as P

F32 = jnp.float32
BF16 = jnp.bfloat16


def twiddles(nlon, modes):
    phase = np.arange(nlon)[:, None] * np.arange(modes)[None, :] % nlon
    angle = phase * (2.0 * math.pi / nlon)
    scale = 1.0 / math.sqrt(nlon)
    return np.stack([np.cos(angle) * scale, -np.sin(angle) * scale]).astype(BF16)


def position(shift, k, sizes):
    owner = lax.rem(lax.axis_index("lat") + shift, sizes["lat"])
    return (owner * sizes["sub"] + lax.axis_index("sub")) * sizes["per"] + k


def owned_row(owner_ref, sizes, shifts):
    lane = lax.broadcasted_iota(jnp.int32, (1, 128), 1)
    row = jnp.full((1, 128), -1, jnp.int32)
    j = 0
    for shift in shifts:
        base = position(shift, 0, sizes)
        for k in range(sizes["per"]):
            row = jnp.where(lane == j, owner_ref[base + k], row)
            j += 1
    return row


def dft_kernel(sizes, step, owner_ref, table_ref, field_ref, *refs):
    *outs, grid_values, chosen, arrived = refs
    per = sizes["per"]
    rows, chans, nlon = grid_values.shape

    def part_copy(i):
        part = pl.ds(i * step, step)
        return pltpu.make_async_copy(field_ref.at[part], grid_values.at[part], arrived.at[i])

    for i in range(rows // step):
        part_copy(i).start()

    row = owned_row(owner_ref, sizes, range(sizes["lat"]))
    modes = table_ref.shape[2]
    pick = (lax.broadcasted_iota(jnp.int32, (modes, 128), 0) == row).astype(F32).astype(BF16)
    for r in range(2):
        chosen[:, r * 128 : (r + 1) * 128] = jnp.dot(
            table_ref[r], pick, preferred_element_type=F32
        ).astype(BF16)

    @pl.loop(0, rows // step)
    def _(i):
        part_copy(i).wait()
        values = grid_values[pl.ds(i * step, step)].reshape(step * chans, nlon).astype(BF16)
        spectrum = jnp.dot(values, chosen[...], preferred_element_type=F32)
        for t in range(step):
            part = spectrum[t * chans : (t + 1) * chans]
            turned = jnp.concatenate([part[:, :128], part[:, 128:]], axis=0).T
            for shift in range(sizes["lat"]):
                outs[shift][i * step + t] = turned[shift * per : (shift + 1) * per].astype(BF16)


def dft(field, ownership, sizes):
    lat_rows, chans, nlon = field.shape
    modes = ownership.shape[0]
    step = 4
    per = sizes["per"]
    table = jnp.asarray(twiddles(nlon, modes))
    vmem = pl.BlockSpec(memory_space=pltpu.VMEM)
    return pl.pallas_call(
        functools.partial(dft_kernel, sizes, step),
        in_specs=[
            pl.BlockSpec(memory_space=pltpu.SMEM),
            vmem,
            pl.BlockSpec(memory_space=pl.ANY),
        ],
        out_specs=[vmem] * sizes["lat"],
        out_shape=[jax.ShapeDtypeStruct((lat_rows, per, 128), BF16)] * sizes["lat"],
        scratch_shapes=[
            pltpu.VMEM(field.shape, F32),
            pltpu.VMEM((nlon, 256), BF16),
            pltpu.SemaphoreType.DMA((lat_rows // step,)),
        ],
        compiler_params=pltpu.CompilerParams(vmem_limit_bytes=52 << 20),
        cost_estimate=pl.CostEstimate(
            flops=2 * lat_rows * chans * nlon * 256, bytes_accessed=field.size * 4, transcendentals=0
        ),
        name="dft",
    )(ownership, table, field)


def pick_kernel(sizes, shifts, owner_ref, legendre_ref, *outs):
    per = sizes["per"]
    row = owned_row(owner_ref, sizes, shifts) - lax.axis_index("sub") * legendre_ref.shape[1]
    pick = (lax.broadcasted_iota(jnp.int32, (legendre_ref.shape[1], 128), 0) == row).astype(F32)
    pick = pick.T[: len(shifts) * per].astype(BF16)
    for t in range(legendre_ref.shape[0]):
        rows = jnp.dot(pick, legendre_ref[t], preferred_element_type=F32)
        for i in range(len(shifts)):
            outs[i][t] = rows[i * per : (i + 1) * per].astype(BF16)


def pick_rows(table, ownership, sizes, shifts, rows):
    _, slab, degrees = table.shape
    per = sizes["per"]
    return pl.pallas_call(
        functools.partial(pick_kernel, sizes, shifts),
        grid=(1,),
        in_specs=[
            pl.BlockSpec(memory_space=pltpu.SMEM),
            pl.BlockSpec(
                (rows, slab, degrees),
                lambda i: (lax.axis_index("rep") * sizes["ch"] + lax.axis_index("ch"), 0, 0),
            ),
        ],
        out_specs=[pl.BlockSpec((rows, per, degrees), lambda i: (0, 0, 0))] * len(shifts),
        out_shape=[jax.ShapeDtypeStruct((rows, per, degrees), BF16)] * len(shifts),
        compiler_params=pltpu.CompilerParams(vmem_limit_bytes=60 << 20),
        cost_estimate=pl.CostEstimate(
            flops=2 * rows * slab * degrees * per * len(shifts),
            bytes_accessed=rows * slab * degrees * 2,
            transcendentals=0,
        ),
        name="pick_rows",
    )(ownership, table)


def pack_kernel(*refs):
    *parts, out_ref = refs
    rows = parts[0].shape[0]
    for i, part in enumerate(parts):
        out_ref[i * rows : (i + 1) * rows] = part[...]


def pack(parts):
    rows, per, width = parts[0].shape
    return pl.pallas_call(
        pack_kernel,
        out_shape=jax.ShapeDtypeStruct((len(parts) * rows, per, width), BF16),
        compiler_params=pltpu.CompilerParams(vmem_limit_bytes=16 << 20),
        name="pack",
    )(*parts)


def by_mode(rows, per, out_ref, scratch):
    depth = out_ref.shape[1]
    for i in range(scratch.shape[0]):
        scratch[i, : depth * per, :] = rows[:, i * 128 : (i + 1) * 128]
    for k in range(per):
        for i in range(scratch.shape[0]):
            out_ref[k, :, i * 128 : (i + 1) * 128] = scratch[
                i, pl.ds(k, depth, stride=per), :
            ].astype(BF16)


def widened(rows, before, after):
    blank = jnp.zeros((after - before, rows.shape[1]), F32)
    parts = []
    for i in range(rows.shape[0] // before):
        parts += [rows[i * before : (i + 1) * before], blank]
    return jnp.concatenate(parts, axis=0)


def own_kernel(sizes, deep, owner_ref, legendre_ref, out_ref, picked, scratch):
    per = sizes["per"]
    lat_rows, slab, degrees = legendre_ref.shape
    share = lat_rows // (sizes["rep"] * sizes["ch"])
    row = owned_row(owner_ref, sizes, (0,)) - lax.axis_index("sub") * slab
    pick = (lax.broadcasted_iota(jnp.int32, (slab, 128), 0) == row).astype(F32)
    pick = pick.T[:per].astype(BF16)
    for t in range(lat_rows):
        picked[t * per : (t + 1) * per, :] = jnp.dot(pick, legendre_ref[t], preferred_element_type=F32)
    by_mode(widened(picked[...], share * per, deep * per), per, out_ref, scratch)


def own_table(by_latitude, ownership, deep, sizes):
    lat_rows, _, degrees = by_latitude.shape
    per = sizes["per"]
    depth = sizes["rep"] * sizes["ch"] * deep
    vmem = pl.BlockSpec(memory_space=pltpu.VMEM)
    return pl.pallas_call(
        functools.partial(own_kernel, sizes, deep),
        in_specs=[pl.BlockSpec(memory_space=pltpu.SMEM), vmem],
        out_specs=vmem,
        out_shape=jax.ShapeDtypeStruct((per, depth, degrees), BF16),
        scratch_shapes=[
            pltpu.VMEM((lat_rows * per, degrees), F32),
            pltpu.VMEM((degrees // 128, depth * per, 128), F32),
        ],
        compiler_params=pltpu.CompilerParams(vmem_limit_bytes=32 << 20),
        cost_estimate=pl.CostEstimate(flops=1000, bytes_accessed=1000, transcendentals=0),
        name="own_table",
    )(ownership, by_latitude)


def turn_kernel(share, deep, rows_ref, out_ref, scratch):
    rows, per, width = rows_ref.shape
    values = rows_ref[...].astype(F32).reshape(rows * per, width)
    by_mode(widened(values, share * per, deep * per), per, out_ref, scratch)


def turn(rows, share, deep):
    total, per, degrees = rows.shape
    depth = total // share * deep
    return pl.pallas_call(
        functools.partial(turn_kernel, share, deep),
        out_shape=jax.ShapeDtypeStruct((per, depth, degrees), BF16),
        scratch_shapes=[pltpu.VMEM((degrees // 128, depth * per, 128), F32)],
        compiler_params=pltpu.CompilerParams(vmem_limit_bytes=16 << 20),
        cost_estimate=pl.CostEstimate(flops=3_000_000_000, bytes_accessed=1000, transcendentals=0),
        name="turn",
    )(rows)


def mix_kernel(sizes, shifts, deep, near_ref, far_ref, w_near, w_far, out_ref, scratch):
    rows, per, width = near_ref.shape
    plane = sizes["rep"] * sizes["ch"]
    lat_rows = rows // len(shifts)
    share = lat_rows // plane
    q = lax.axis_index("rep") * sizes["ch"] + lax.axis_index("ch")
    nt = (((1,), (1,)), ((), ()))
    parts = []
    for i, shift in enumerate(shifts):
        for d in range(plane):
            at = d if shift == 0 else jnp.bitwise_xor(q, d)
            part = pl.ds(i * lat_rows + at * share, share)
            a = near_ref[part].reshape(share * per, width)
            b = far_ref[part].reshape(share * per, width)
            mixed = lax.dot_general(a, w_near[...], nt, preferred_element_type=F32)
            mixed += lax.dot_general(b, w_far[...], nt, preferred_element_type=F32)
            parts.append(widened(mixed, share * per, deep * per))
    by_mode(jnp.concatenate(parts, axis=0), per, out_ref, scratch)


def mix(near, far, w_near, w_far, shifts, deep, sizes):
    rows, per, width = near.shape
    depth = len(shifts) * sizes["rep"] * sizes["ch"] * deep
    return pl.pallas_call(
        functools.partial(mix_kernel, sizes, shifts, deep),
        out_shape=jax.ShapeDtypeStruct((per, depth, width), BF16),
        scratch_shapes=[pltpu.VMEM((1, depth * per, width), F32)],
        compiler_params=pltpu.CompilerParams(vmem_limit_bytes=16 << 20),
        cost_estimate=pl.CostEstimate(
            flops=400 * 2 * near.size * width, bytes_accessed=near.size * 4, transcendentals=0
        ),
        name="mix",
    )(near, far, w_near, w_far)


def cross_kernel(near_ref, far_ref, w_near, w_far, *outs):
    rows, per, width = near_ref.shape
    lat_rows = rows // len(outs)
    nt = (((1,), (1,)), ((), ()))
    for i, out_ref in enumerate(outs):
        part = slice(i * lat_rows, (i + 1) * lat_rows)
        a = near_ref[part].reshape(lat_rows * per, width)
        b = far_ref[part].reshape(lat_rows * per, width)
        mixed = lax.dot_general(a, w_near[...], nt, preferred_element_type=F32)
        mixed += lax.dot_general(b, w_far[...], nt, preferred_element_type=F32)
        out_ref[...] = mixed.astype(BF16).reshape(lat_rows, per, width)


def cross_parts(near, far, w_near, w_far, parts):
    rows, per, width = near.shape
    return pl.pallas_call(
        cross_kernel,
        out_shape=[jax.ShapeDtypeStruct((rows // parts, per, width), BF16)] * parts,
        compiler_params=pltpu.CompilerParams(vmem_limit_bytes=16 << 20),
        cost_estimate=pl.CostEstimate(flops=1_000_000_000, bytes_accessed=1000, transcendentals=0),
        name="cross",
    )(near, far, w_near, w_far)


def arrange_kernel(sizes, shift, deep, rows_ref, out_ref, scratch):
    lat_rows, per, width = rows_ref.shape
    plane = sizes["rep"] * sizes["ch"]
    share = lat_rows // plane
    q = lax.axis_index("rep") * sizes["ch"] + lax.axis_index("ch")
    parts = []
    for d in range(plane):
        at = d if shift == 0 else jnp.bitwise_xor(q, d)
        part = rows_ref[pl.ds(at * share, share)].astype(F32).reshape(share * per, width)
        parts.append(widened(part, share * per, deep * per))
    by_mode(jnp.concatenate(parts, axis=0), per, out_ref, scratch)


def arrange(rows, shift, deep, sizes):
    _, per, width = rows.shape
    depth = sizes["rep"] * sizes["ch"] * deep
    return pl.pallas_call(
        functools.partial(arrange_kernel, sizes, shift, deep),
        out_shape=jax.ShapeDtypeStruct((per, depth, width), BF16),
        scratch_shapes=[pltpu.VMEM((1, depth * per, width), F32)],
        compiler_params=pltpu.CompilerParams(vmem_limit_bytes=16 << 20),
        cost_estimate=pl.CostEstimate(flops=2_000_000_000, bytes_accessed=1000, transcendentals=0),
        name="arrange",
    )(rows)


def contract_kernel(lats, plane, group, *refs):
    *spectra, own = refs[: -plane - 1]
    *tables, out_ref = refs[-plane - 1 :]
    deep = own.shape[1] // plane
    half = out_ref.shape[2]
    for k in range(group):
        a = jnp.concatenate([part[k] for part in spectra], axis=0)
        pieces = [own[k]]
        for s in range(lats - 1):
            pieces += [table[k, s * deep : (s + 1) * deep] for table in tables]
        b = jnp.concatenate(pieces, axis=0)
        c = lax.dot_general(a, b, (((0,), (0,)), ((), ())), preferred_element_type=F32)
        out_ref[0, k] = c[:half].astype(BF16)
        out_ref[1, k] = c[half:].astype(BF16)


def contract(spectra, own, tables, lats):
    per, _, width = spectra[0].shape
    degrees = own.shape[2]
    group = 8
    block = lambda x: pl.BlockSpec((group, *x.shape[1:]), lambda i: (i, 0, 0))
    return pl.pallas_call(
        functools.partial(contract_kernel, lats, len(tables), group),
        grid=(per // group,),
        in_specs=[block(x) for x in (*spectra, own, *tables)],
        out_specs=pl.BlockSpec((2, group, width // 2, degrees), lambda i: (0, i, 0, 0)),
        out_shape=jax.ShapeDtypeStruct((2, per, width // 2, degrees), BF16),
        compiler_params=pltpu.CompilerParams(vmem_limit_bytes=40 << 20),
        name="contract",
    )(*spectra, own, *tables)


def mixing_weights(w_real, w_imag):
    half = w_real.shape[0]
    x = lax.axis_index("ch")
    out = []
    for side in (x, 1 - x):
        wr = lax.dynamic_slice_in_dim(w_real, side * half, half, 1)
        wi = lax.dynamic_slice_in_dim(w_imag, side * half, half, 1)
        out.append(
            jnp.concatenate(
                [jnp.concatenate([wr, -wi], axis=1), jnp.concatenate([wi, wr], axis=1)], axis=0
            )
        )
    return out


def fast(field, legendre, ownership, w_real, w_imag, sizes):
    lats, plane = sizes["lat"], sizes["rep"] * sizes["ch"]
    lat_rows = field.shape[0]
    share, deep = lat_rows // plane, (lat_rows // plane + 7) // 8 * 8
    by_latitude = jnp.transpose(legendre, (1, 0, 2))
    forward = lambda v, s: lax.ppermute(v, "lat", [(i, (i + s) % lats) for i in range(lats)])
    across = lambda v: lax.ppermute(v, "ch", [(0, 1), (1, 0)])
    beyond = lambda v: lax.ppermute(v, "rep", [(0, 1), (1, 0)])
    after = lambda v, *before: lax.optimization_barrier((v, *before))[0]
    others = tuple(range(1, lats))
    sent = pick_rows(by_latitude, ownership, sizes, others, share)
    landed = [forward(v, s) for s, v in zip(others, sent)]
    spectra = dft(field, after(ownership, sent[0]), sizes)
    w_near, w_far = mixing_weights(w_real, w_imag)
    own = own_table(by_latitude, ownership, deep, sizes)
    mine = pack(landed)
    beside = across(mine)
    beyond_mine = beyond(mine)
    early = pack([spectra[0], spectra[1]])
    far_early = across(early)
    near2 = forward(spectra[2], 2)
    near3 = forward(spectra[3], 3)
    zero, *sums = cross_parts(early, far_early, w_near, w_far, 2)
    mixed = [arrange(zero, 0, deep, sizes)]
    sum1 = forward(sums[0], 1)
    late = pack([near2, near3])
    beyond_beside = beyond(beside)
    far_late = across(after(late, sums[0]))
    tables = [turn(v, share, deep) for v in (mine, beside, beyond_mine, beyond_beside)]
    mixed_late = mix(late, far_late, w_near, w_far, (2, 3), deep, sizes)
    mixed += [arrange(sum1, 1, deep, sizes), mixed_late]
    return contract(mixed, own, tables, lats)


def fourier_rows(flat_field, modes, lat_rows, chans, nlon):
    longitude = jnp.arange(nlon, dtype=jnp.int32)
    phase = longitude[:, None] * modes[None, :] % nlon
    angle = phase.astype(jnp.float32) * (2.0 * math.pi / nlon)
    scale = 1.0 / math.sqrt(nlon)
    real_part = (
        jnp.dot(
            flat_field,
            jnp.cos(angle),
            precision=lax.Precision.HIGHEST,
            preferred_element_type=jnp.float32,
        )
        * scale
    )
    imag_part = (
        -jnp.dot(
            flat_field,
            jnp.sin(angle),
            precision=lax.Precision.HIGHEST,
            preferred_element_type=jnp.float32,
        )
        * scale
    )
    both = jnp.stack([real_part, imag_part]).reshape(2, lat_rows, chans, modes.shape[0])
    both = jnp.transpose(both, (3, 1, 0, 2)).reshape(modes.shape[0], lat_rows, 2 * chans)
    return both.astype(jnp.bfloat16)


def general(field, legendre, ownership, w_real, w_imag):
    lat_rows, chans, nlon = field.shape
    degrees = legendre.shape[2]
    slab_modes = legendre.shape[0]
    blocks = lax.axis_size("lat")
    halves = lax.axis_size("sub")
    per_block = ownership.shape[0] // (blocks * halves)
    my_modes = lax.dynamic_index_in_dim(
        ownership.reshape(blocks, halves, per_block), lax.axis_index("sub"), 1, keepdims=False
    ).reshape(blocks * per_block)
    slab_index = my_modes - lax.axis_index("sub") * slab_modes
    flat_field = field.reshape(lat_rows * chans, nlon)
    spectra_rows = fourier_rows(flat_field, my_modes, lat_rows, chans, nlon)
    table_rows = jnp.take(legendre, slab_index, axis=0)
    spectra_all, tables_all = (
        lax.all_to_all(spectra_rows, "lat", split_axis=0, concat_axis=1, tiled=True),
        lax.all_to_all(table_rows, "lat", split_axis=0, concat_axis=1, tiled=True),
    )
    spectra_all = spectra_all.reshape(per_block, blocks, lat_rows, 2 * chans)
    tables_all = tables_all.reshape(per_block, blocks, lat_rows, degrees)
    block_part = jnp.einsum(
        "kbtc,kbtl->kbcl", spectra_all, tables_all, preferred_element_type=jnp.float32
    )
    total = jnp.sum(block_part, axis=1)
    coeff = total.astype(jnp.bfloat16).reshape(per_block, 2, chans, degrees)
    piece = lax.all_gather(coeff, "ch", axis=2, tiled=True)
    real_in = piece[:, 0]
    imag_in = piece[:, 1]
    real_out = jnp.einsum(
        "oc,kcl->kol", w_real, real_in, preferred_element_type=jnp.float32
    ) - jnp.einsum("oc,kcl->kol", w_imag, imag_in, preferred_element_type=jnp.float32)
    imag_out = jnp.einsum(
        "oc,kcl->kol", w_real, imag_in, preferred_element_type=jnp.float32
    ) + jnp.einsum("oc,kcl->kol", w_imag, real_in, preferred_element_type=jnp.float32)
    mixed = jnp.stack([real_out, imag_out])
    return mixed.astype(jnp.bfloat16)


def per_device(sizes, field, legendre, ownership, w_real, w_imag):
    lat_rows, chans, nlon = field.shape
    sizes = dict(sizes, per=ownership.shape[0] // (sizes["lat"] * sizes["sub"]))
    plane = sizes["rep"] * sizes["ch"]
    fits = (
        sizes["ch"] == 2
        and sizes["rep"] == 2
        and sizes["lat"] == 4
        and 2 * chans == 128
        and lat_rows % plane == 0
        and lat_rows % 4 == 0
        and sizes["per"] % 8 == 0
        and sizes["lat"] * sizes["per"] <= 128
        and legendre.shape[2] % 128 == 0
    )
    if fits:
        return fast(field, legendre, ownership, w_real, w_imag, sizes)
    return general(field, legendre, ownership, w_real, w_imag)


def solution(mesh):
    in_specs = (
        P(("rep", "lat"), "ch", None),
        P("sub", "lat", None),
        P(),
        P("ch", None),
        P("ch", None),
    )
    out_specs = P("rep", ("lat", "sub"), "ch", None)
    return jax.shard_map(
        functools.partial(per_device, dict(mesh.shape)),
        mesh=mesh,
        in_specs=in_specs,
        out_specs=out_specs,
        check_vma=False,
    )
```

```python
import functools
import math

import jax
import jax.numpy as jnp
import numpy as np
from jax import lax
from jax.experimental import pallas as pl
from jax.experimental.pallas import tpu as pltpu
from jax.sharding import PartitionSpec as P

F32 = jnp.float32
BF16 = jnp.bfloat16


def twiddles(nlon, modes, parts):
    phase = np.arange(nlon)[:, None] * np.arange(modes)[None, :] % nlon
    angle = phase * (2.0 * math.pi / nlon)
    scale = 1.0 / math.sqrt(nlon)
    waves = np.stack([np.cos(angle) * scale, -np.sin(angle) * scale]).astype(BF16)
    return np.moveaxis(waves.reshape(2, nlon, parts, modes // parts), 2, 0).copy()


def position(shift, k, sizes):
    owner = lax.rem(lax.axis_index("lat") + shift, sizes["lat"])
    return (owner * sizes["sub"] + lax.axis_index("sub")) * sizes["per"] + k


def owned_row(owner_ref, sizes, shifts):
    lane = lax.broadcasted_iota(jnp.int32, (1, 128), 1)
    row = jnp.full((1, 128), -1, jnp.int32)
    j = 0
    for shift in shifts:
        base = position(shift, 0, sizes)
        for k in range(sizes["per"]):
            row = jnp.where(lane == j, owner_ref[base + k], row)
            j += 1
    return row


def choice(modes_ref, slab):
    row = lax.broadcasted_iota(jnp.int32, (slab, 128), 0)
    return (row == modes_ref[:1]).astype(F32)


def dft_kernel(sizes, step, ahead, modes_ref, table_ref, field_ref, *refs):
    *outs, grid_values, chosen, arrived = refs
    per = sizes["per"]
    rows, chans, nlon = grid_values.shape
    steps = rows // step

    def part_copy(i):
        part = pl.ds(i * step, step)
        return pltpu.make_async_copy(field_ref.at[part], grid_values.at[part], arrived.at[i])

    for i in range(ahead):
        part_copy(i).start()

    pick = choice(modes_ref, table_ref.shape[2]).astype(BF16)
    for r in range(2):
        chosen[:, r * 128 : (r + 1) * 128] = jnp.dot(
            table_ref[r], pick, preferred_element_type=F32
        ).astype(BF16)

    @pl.loop(0, steps)
    def _(i):
        part_copy(i).wait()

        @pl.when(i + ahead < steps)
        def _():
            part_copy(i + ahead).start()

        values = grid_values[pl.ds(i * step, step)].reshape(step * chans, nlon).astype(BF16)
        spectrum = jnp.dot(values, chosen[...], preferred_element_type=F32)
        for t in range(step):
            part = spectrum[t * chans : (t + 1) * chans]
            turned = jnp.concatenate([part[:, :128], part[:, 128:]], axis=0).T
            for shift in range(sizes["lat"]):
                outs[shift][i * step + t] = turned[shift * per : (shift + 1) * per].astype(BF16)


def dft(field, modes, sizes):
    lat_rows, chans, nlon = field.shape
    per, step, ahead = sizes["per"], 4, 7
    slab = sizes["lat"] * per
    waves = jnp.asarray(twiddles(nlon, slab * sizes["sub"], sizes["sub"]))
    table = lax.dynamic_index_in_dim(waves, lax.axis_index("sub"), 0, keepdims=False)
    held = pl.BlockSpec(memory_space=pl.ANY)
    vmem = pl.BlockSpec(memory_space=pltpu.VMEM)
    return pl.pallas_call(
        functools.partial(dft_kernel, sizes, step, ahead),
        in_specs=[vmem, vmem, held],
        out_specs=[vmem] * sizes["lat"],
        out_shape=[jax.ShapeDtypeStruct((lat_rows, per, 128), BF16)] * sizes["lat"],
        scratch_shapes=[
            pltpu.VMEM(field.shape, F32),
            pltpu.VMEM((nlon, 256), BF16),
            pltpu.SemaphoreType.DMA((lat_rows // step,)),
        ],
        compiler_params=pltpu.CompilerParams(vmem_limit_bytes=48 << 20),
        cost_estimate=pl.CostEstimate(
            flops=2 * lat_rows * chans * nlon * 256, bytes_accessed=field.size * 4, transcendentals=0
        ),
        name="dft",
    )(modes, table, field)


def pick_kernel(sizes, ownership_ref, table_ref, modes_ref, *refs):
    *outs, legendre_ref, owner_ref, arrived, known = refs
    per = sizes["per"]
    rows, slab, _ = legendre_ref.shape
    share = lax.axis_index("rep") * sizes["ch"] + lax.axis_index("ch")
    owners = pltpu.make_async_copy(ownership_ref, owner_ref, known)
    owners.start()
    values = pltpu.make_async_copy(table_ref.at[pl.ds(share * rows, rows)], legendre_ref, arrived)
    values.start()
    owners.wait()
    row = owned_row(owner_ref, sizes, range(sizes["lat"])) - lax.axis_index("sub") * slab
    modes_ref[...] = jnp.broadcast_to(row, modes_ref.shape)
    pick = choice(modes_ref, slab).T[per : sizes["lat"] * per].astype(BF16)
    values.wait()
    for t in range(rows):
        picked = jnp.dot(pick, legendre_ref[t], preferred_element_type=F32)
        for i, out_ref in enumerate(outs):
            out_ref[t] = picked[i * per : (i + 1) * per].astype(BF16)


def pick_rows(table, ownership, sizes, rows):
    _, slab, degrees = table.shape
    per, others = sizes["per"], sizes["lat"] - 1
    held = pl.BlockSpec(memory_space=pl.ANY)
    return pl.pallas_call(
        functools.partial(pick_kernel, sizes),
        in_specs=[held, held],
        out_specs=[pl.BlockSpec(memory_space=pltpu.VMEM)] * (1 + others),
        out_shape=[jax.ShapeDtypeStruct((8, 128), jnp.int32)]
        + [jax.ShapeDtypeStruct((rows, per, degrees), BF16)] * others,
        scratch_shapes=[
            pltpu.VMEM((rows, slab, degrees), BF16),
            pltpu.SMEM(ownership.shape, jnp.int32),
            pltpu.SemaphoreType.DMA,
            pltpu.SemaphoreType.DMA,
        ],
        compiler_params=pltpu.CompilerParams(vmem_limit_bytes=62 * 1000 * 1000),
        cost_estimate=pl.CostEstimate(
            flops=2 * rows * slab * degrees * per * others,
            bytes_accessed=rows * slab * degrees * 2,
            transcendentals=0,
        ),
        name="pick_rows",
    )(ownership, table)


def pack_kernel(*refs):
    *parts, out_ref = refs
    rows = parts[0].shape[0]
    for i, part in enumerate(parts):
        out_ref[i * rows : (i + 1) * rows] = part[...]


def pack(parts):
    rows, per, width = parts[0].shape
    return pl.pallas_call(
        pack_kernel,
        out_shape=jax.ShapeDtypeStruct((len(parts) * rows, per, width), BF16),
        compiler_params=pltpu.CompilerParams(vmem_limit_bytes=16 << 20),
        name="pack",
    )(*parts)


def by_mode(rows, per, out_ref, scratch):
    depth = out_ref.shape[1]
    for i in range(scratch.shape[0]):
        scratch[i, : depth * per, :] = rows[:, i * 128 : (i + 1) * 128]
    for k in range(per):
        for i in range(scratch.shape[0]):
            out_ref[k, :, i * 128 : (i + 1) * 128] = scratch[
                i, pl.ds(k, depth, stride=per), :
            ].astype(BF16)


def widened(rows, before, after):
    blank = jnp.zeros((after - before, rows.shape[1]), F32)
    parts = []
    for i in range(rows.shape[0] // before):
        parts += [rows[i * before : (i + 1) * before], blank]
    return jnp.concatenate(parts, axis=0)


def own_kernel(sizes, deep, modes_ref, legendre_ref, out_ref, picked, scratch):
    per = sizes["per"]
    lat_rows, slab, degrees = legendre_ref.shape
    share = lat_rows // (sizes["rep"] * sizes["ch"])
    pick = choice(modes_ref, slab).T[:per].astype(BF16)
    for t in range(lat_rows):
        picked[t * per : (t + 1) * per, :] = jnp.dot(pick, legendre_ref[t], preferred_element_type=F32)
    by_mode(widened(picked[...], share * per, deep * per), per, out_ref, scratch)


def own_table(by_latitude, modes, deep, sizes):
    lat_rows, _, degrees = by_latitude.shape
    per = sizes["per"]
    depth = sizes["rep"] * sizes["ch"] * deep
    vmem = pl.BlockSpec(memory_space=pltpu.VMEM)
    return pl.pallas_call(
        functools.partial(own_kernel, sizes, deep),
        in_specs=[vmem, vmem],
        out_specs=vmem,
        out_shape=jax.ShapeDtypeStruct((per, depth, degrees), BF16),
        scratch_shapes=[
            pltpu.VMEM((lat_rows * per, degrees), F32),
            pltpu.VMEM((degrees // 128, depth * per, 128), F32),
        ],
        compiler_params=pltpu.CompilerParams(vmem_limit_bytes=32 << 20),
        cost_estimate=pl.CostEstimate(flops=3_000_000_000, bytes_accessed=1000, transcendentals=0),
        name="own_table",
    )(modes, by_latitude)


def turn_kernel(share, deep, rows_ref, out_ref, scratch):
    rows, per, width = rows_ref.shape
    values = rows_ref[...].astype(F32).reshape(rows * per, width)
    by_mode(widened(values, share * per, deep * per), per, out_ref, scratch)


def turn(rows, share, deep):
    total, per, degrees = rows.shape
    depth = total // share * deep
    return pl.pallas_call(
        functools.partial(turn_kernel, share, deep),
        out_shape=jax.ShapeDtypeStruct((per, depth, degrees), BF16),
        scratch_shapes=[pltpu.VMEM((degrees // 128, depth * per, 128), F32)],
        compiler_params=pltpu.CompilerParams(vmem_limit_bytes=16 << 20),
        cost_estimate=pl.CostEstimate(flops=1000, bytes_accessed=1000, transcendentals=0),
        name="turn",
    )(rows)


def mix_kernel(sizes, shifts, deep, near_ref, far_ref, w_near, w_far, out_ref, scratch):
    rows, per, width = near_ref.shape
    plane = sizes["rep"] * sizes["ch"]
    lat_rows = rows // len(shifts)
    share = lat_rows // plane
    q = lax.axis_index("rep") * sizes["ch"] + lax.axis_index("ch")
    nt = (((1,), (1,)), ((), ()))
    parts = []
    for i, shift in enumerate(shifts):
        for d in range(plane):
            at = d if shift == 0 else jnp.bitwise_xor(q, d)
            part = pl.ds(i * lat_rows + at * share, share)
            a = near_ref[part].reshape(share * per, width)
            b = far_ref[part].reshape(share * per, width)
            mixed = lax.dot_general(a, w_near[...], nt, preferred_element_type=F32)
            mixed += lax.dot_general(b, w_far[...], nt, preferred_element_type=F32)
            parts.append(widened(mixed, share * per, deep * per))
    by_mode(jnp.concatenate(parts, axis=0), per, out_ref, scratch)


def mix(near, far, w_near, w_far, shifts, deep, sizes):
    rows, per, width = near.shape
    depth = len(shifts) * sizes["rep"] * sizes["ch"] * deep
    return pl.pallas_call(
        functools.partial(mix_kernel, sizes, shifts, deep),
        out_shape=jax.ShapeDtypeStruct((per, depth, width), BF16),
        scratch_shapes=[pltpu.VMEM((1, depth * per, width), F32)],
        compiler_params=pltpu.CompilerParams(vmem_limit_bytes=16 << 20),
        cost_estimate=pl.CostEstimate(
            flops=2 * 2 * near.size * width, bytes_accessed=near.size * 4, transcendentals=0
        ),
        name="mix",
    )(near, far, w_near, w_far)


def cross_kernel(near_ref, far_ref, w_near, w_far, *outs):
    rows, per, width = near_ref.shape
    lat_rows = rows // len(outs)
    nt = (((1,), (1,)), ((), ()))
    for i, out_ref in enumerate(outs):
        part = slice(i * lat_rows, (i + 1) * lat_rows)
        a = near_ref[part].reshape(lat_rows * per, width)
        b = far_ref[part].reshape(lat_rows * per, width)
        mixed = lax.dot_general(a, w_near[...], nt, preferred_element_type=F32)
        mixed += lax.dot_general(b, w_far[...], nt, preferred_element_type=F32)
        out_ref[...] = mixed.astype(BF16).reshape(lat_rows, per, width)


def cross_parts(near, far, w_near, w_far, parts):
    rows, per, width = near.shape
    return pl.pallas_call(
        cross_kernel,
        out_shape=[jax.ShapeDtypeStruct((rows // parts, per, width), BF16)] * parts,
        compiler_params=pltpu.CompilerParams(vmem_limit_bytes=16 << 20),
        cost_estimate=pl.CostEstimate(flops=1000, bytes_accessed=1000, transcendentals=0),
        name="cross",
    )(near, far, w_near, w_far)


def arrange_kernel(sizes, shift, deep, rows_ref, out_ref, scratch):
    lat_rows, per, width = rows_ref.shape
    plane = sizes["rep"] * sizes["ch"]
    share = lat_rows // plane
    q = lax.axis_index("rep") * sizes["ch"] + lax.axis_index("ch")
    parts = []
    for d in range(plane):
        at = d if shift == 0 else jnp.bitwise_xor(q, d)
        part = rows_ref[pl.ds(at * share, share)].astype(F32).reshape(share * per, width)
        parts.append(widened(part, share * per, deep * per))
    by_mode(jnp.concatenate(parts, axis=0), per, out_ref, scratch)


def arrange(rows, shift, deep, sizes):
    _, per, width = rows.shape
    depth = sizes["rep"] * sizes["ch"] * deep
    return pl.pallas_call(
        functools.partial(arrange_kernel, sizes, shift, deep),
        out_shape=jax.ShapeDtypeStruct((per, depth, width), BF16),
        scratch_shapes=[pltpu.VMEM((1, depth * per, width), F32)],
        compiler_params=pltpu.CompilerParams(vmem_limit_bytes=16 << 20),
        cost_estimate=pl.CostEstimate(flops=4_000_000_000, bytes_accessed=1000, transcendentals=0),
        name="arrange",
    )(rows)


def contract_kernel(order, plane, group, *refs):
    *spectra, own = refs[: -plane - 1]
    *tables, out_ref = refs[-plane - 1 :]
    deep = own.shape[1] // plane
    half = out_ref.shape[2]
    for k in range(group):
        a = jnp.concatenate([part[k] for part in spectra], axis=0)
        pieces = [own[k]]
        for s in order:
            pieces += [table[k, (s - 1) * deep : s * deep] for table in tables]
        b = jnp.concatenate(pieces, axis=0)
        c = lax.dot_general(a, b, (((0,), (0,)), ((), ())), preferred_element_type=F32)
        out_ref[0, k] = c[:half].astype(BF16)
        out_ref[1, k] = c[half:].astype(BF16)


def contract(spectra, own, tables, order):
    per, _, width = spectra[0].shape
    degrees = own.shape[2]
    group = 12
    block = lambda x: pl.BlockSpec((group, *x.shape[1:]), lambda i: (i, 0, 0))
    return pl.pallas_call(
        functools.partial(contract_kernel, order, len(tables), group),
        grid=(per // group,),
        in_specs=[block(x) for x in (*spectra, own, *tables)],
        out_specs=pl.BlockSpec((2, group, width // 2, degrees), lambda i: (0, i, 0, 0)),
        out_shape=jax.ShapeDtypeStruct((2, per, width // 2, degrees), BF16),
        compiler_params=pltpu.CompilerParams(vmem_limit_bytes=40 << 20),
        name="contract",
    )(*spectra, own, *tables)


def mixing_weights(w_real, w_imag):
    half = w_real.shape[0]
    x = lax.axis_index("ch")
    out = []
    for side in (x, 1 - x):
        wr = lax.dynamic_slice_in_dim(w_real, side * half, half, 1)
        wi = lax.dynamic_slice_in_dim(w_imag, side * half, half, 1)
        out.append(
            jnp.concatenate(
                [jnp.concatenate([wr, -wi], axis=1), jnp.concatenate([wi, wr], axis=1)], axis=0
            )
        )
    return out


def fast(field, legendre, ownership, w_real, w_imag, sizes):
    lats, plane = sizes["lat"], sizes["rep"] * sizes["ch"]
    lat_rows = field.shape[0]
    share, deep = lat_rows // plane, (lat_rows // plane + 7) // 8 * 8
    by_latitude = jnp.transpose(legendre, (1, 0, 2))
    forward = lambda v, s: lax.ppermute(v, "lat", [(i, (i + s) % lats) for i in range(lats)])
    across = lambda v: lax.ppermute(v, "ch", [(0, 1), (1, 0)])
    beyond = lambda v: lax.ppermute(v, "rep", [(0, 1), (1, 0)])
    after = lambda v, *before: lax.optimization_barrier((v, *before))[0]
    modes, *sent = pick_rows(by_latitude, ownership, sizes, share)
    landed = [forward(v, s) for s, v in enumerate(sent, 1)]
    spectra = dft(field, modes, sizes)
    w_near, w_far = mixing_weights(w_real, w_imag)
    own = own_table(by_latitude, modes, deep, sizes)
    mine = pack(landed)
    beside = across(mine)
    beyond_mine = beyond(mine)
    early = pack([spectra[0], spectra[2]])
    far_early = across(early)
    near3 = forward(after(spectra[3], mine), 3)
    near1 = forward(after(spectra[1], mine), 1)
    zero, *sums = cross_parts(early, far_early, w_near, w_far, 2)
    mixed = [arrange(zero, 0, deep, sizes)]
    sum2 = forward(sums[0], 2)
    late0 = pack([near3, near1])
    beyond_beside = beyond(beside)
    far_late0 = across(late0)
    far_late0 = after(far_late0, sum2)
    tables = [turn(v, share, deep) for v in (mine, beside, beyond_mine, beyond_beside)]
    mixed.append(mix(late0, far_late0, w_near, w_far, (3, 1), deep, sizes))
    mixed += [arrange(v, s, deep, sizes) for v, s in ((sum2, 2),)]
    return contract(mixed, own, tables, (3, 1, 2))


def fourier_rows(flat_field, modes, lat_rows, chans, nlon):
    longitude = jnp.arange(nlon, dtype=jnp.int32)
    phase = longitude[:, None] * modes[None, :] % nlon
    angle = phase.astype(jnp.float32) * (2.0 * math.pi / nlon)
    scale = 1.0 / math.sqrt(nlon)
    real_part = (
        jnp.dot(
            flat_field,
            jnp.cos(angle),
            precision=lax.Precision.HIGHEST,
            preferred_element_type=jnp.float32,
        )
        * scale
    )
    imag_part = (
        -jnp.dot(
            flat_field,
            jnp.sin(angle),
            precision=lax.Precision.HIGHEST,
            preferred_element_type=jnp.float32,
        )
        * scale
    )
    both = jnp.stack([real_part, imag_part]).reshape(2, lat_rows, chans, modes.shape[0])
    both = jnp.transpose(both, (3, 1, 0, 2)).reshape(modes.shape[0], lat_rows, 2 * chans)
    return both.astype(jnp.bfloat16)


def general(field, legendre, ownership, w_real, w_imag):
    lat_rows, chans, nlon = field.shape
    degrees = legendre.shape[2]
    slab_modes = legendre.shape[0]
    blocks = lax.axis_size("lat")
    halves = lax.axis_size("sub")
    per_block = ownership.shape[0] // (blocks * halves)
    my_modes = lax.dynamic_index_in_dim(
        ownership.reshape(blocks, halves, per_block), lax.axis_index("sub"), 1, keepdims=False
    ).reshape(blocks * per_block)
    slab_index = my_modes - lax.axis_index("sub") * slab_modes
    flat_field = field.reshape(lat_rows * chans, nlon)
    spectra_rows = fourier_rows(flat_field, my_modes, lat_rows, chans, nlon)
    table_rows = jnp.take(legendre, slab_index, axis=0)
    spectra_all, tables_all = (
        lax.all_to_all(spectra_rows, "lat", split_axis=0, concat_axis=1, tiled=True),
        lax.all_to_all(table_rows, "lat", split_axis=0, concat_axis=1, tiled=True),
    )
    spectra_all = spectra_all.reshape(per_block, blocks, lat_rows, 2 * chans)
    tables_all = tables_all.reshape(per_block, blocks, lat_rows, degrees)
    block_part = jnp.einsum(
        "kbtc,kbtl->kbcl", spectra_all, tables_all, preferred_element_type=jnp.float32
    )
    total = jnp.sum(block_part, axis=1)
    coeff = total.astype(jnp.bfloat16).reshape(per_block, 2, chans, degrees)
    piece = lax.all_gather(coeff, "ch", axis=2, tiled=True)
    real_in = piece[:, 0]
    imag_in = piece[:, 1]
    real_out = jnp.einsum(
        "oc,kcl->kol", w_real, real_in, preferred_element_type=jnp.float32
    ) - jnp.einsum("oc,kcl->kol", w_imag, imag_in, preferred_element_type=jnp.float32)
    imag_out = jnp.einsum(
        "oc,kcl->kol", w_real, imag_in, preferred_element_type=jnp.float32
    ) + jnp.einsum("oc,kcl->kol", w_imag, real_in, preferred_element_type=jnp.float32)
    mixed = jnp.stack([real_out, imag_out])
    return mixed.astype(jnp.bfloat16)


def per_device(sizes, field, legendre, ownership, w_real, w_imag):
    lat_rows, chans, nlon = field.shape
    sizes = dict(sizes, per=ownership.shape[0] // (sizes["lat"] * sizes["sub"]))
    plane = sizes["rep"] * sizes["ch"]
    fits = (
        sizes["ch"] == 2
        and sizes["rep"] == 2
        and sizes["lat"] == 4
        and 2 * chans == 128
        and lat_rows % plane == 0
        and lat_rows % 28 == 0
        and sizes["per"] % 8 == 0
        and sizes["lat"] * sizes["per"] <= 128
        and legendre.shape[2] % 128 == 0
    )
    if fits:
        return fast(field, legendre, ownership, w_real, w_imag, sizes)
    return general(field, legendre, ownership, w_real, w_imag)


def solution(mesh):
    in_specs = (
        P(("rep", "lat"), "ch", None),
        P("sub", "lat", None),
        P(),
        P("ch", None),
        P("ch", None),
    )
    out_specs = P("rep", ("lat", "sub"), "ch", None)
    return jax.shard_map(
        functools.partial(per_device, dict(mesh.shape)),
        mesh=mesh,
        in_specs=in_specs,
        out_specs=out_specs,
        check_vma=False,
    )
```

```python
import functools
import math

import jax
import jax.numpy as jnp
import numpy as np
from jax import lax
from jax.experimental import pallas as pl
from jax.experimental.pallas import tpu as pltpu
from jax.sharding import PartitionSpec as P

F32 = jnp.float32
BF16 = jnp.bfloat16


def twiddles(nlon, modes, parts):
    phase = np.arange(nlon)[:, None] * np.arange(modes)[None, :] % nlon
    angle = phase * (2.0 * math.pi / nlon)
    scale = 1.0 / math.sqrt(nlon)
    waves = np.stack([np.cos(angle) * scale, -np.sin(angle) * scale]).astype(BF16)
    return np.moveaxis(waves.reshape(2, nlon, parts, modes // parts), 2, 0).copy()


def position(shift, k, sizes):
    owner = lax.rem(lax.axis_index("lat") + shift, sizes["lat"])
    return (owner * sizes["sub"] + lax.axis_index("sub")) * sizes["per"] + k


def owned_row(owner_ref, sizes, shifts):
    lane = lax.broadcasted_iota(jnp.int32, (1, 128), 1)
    row = jnp.full((1, 128), -1, jnp.int32)
    j = 0
    for shift in shifts:
        base = position(shift, 0, sizes)
        for k in range(sizes["per"]):
            row = jnp.where(lane == j, owner_ref[base + k], row)
            j += 1
    return row


def choice(modes_ref, slab):
    row = lax.broadcasted_iota(jnp.int32, (slab, 128), 0)
    return (row == modes_ref[:1]).astype(F32)


def dft_kernel(sizes, step, ahead, modes_ref, table_ref, field_ref, *refs):
    *outs, grid_values, chosen, arrived = refs
    per = sizes["per"]
    rows, chans, nlon = grid_values.shape
    steps = rows // step

    def part_copy(i):
        part = pl.ds(i * step, step)
        return pltpu.make_async_copy(field_ref.at[part], grid_values.at[part], arrived.at[i])

    for i in range(ahead):
        part_copy(i).start()

    pick = choice(modes_ref, table_ref.shape[2]).astype(BF16)
    for r in range(2):
        chosen[:, r * 128 : (r + 1) * 128] = jnp.dot(
            table_ref[r], pick, preferred_element_type=F32
        ).astype(BF16)

    @pl.loop(0, steps)
    def _(i):
        part_copy(i).wait()

        @pl.when(i + ahead < steps)
        def _():
            part_copy(i + ahead).start()

        values = grid_values[pl.ds(i * step, step)].reshape(step * chans, nlon).astype(BF16)
        spectrum = jnp.dot(values, chosen[...], preferred_element_type=F32)
        for t in range(step):
            part = spectrum[t * chans : (t + 1) * chans]
            turned = jnp.concatenate([part[:, :128], part[:, 128:]], axis=0).T
            for shift in range(sizes["lat"]):
                outs[shift][i * step + t] = turned[shift * per : (shift + 1) * per].astype(BF16)


def dft(field, modes, sizes):
    lat_rows, chans, nlon = field.shape
    per, step, ahead = sizes["per"], 4, 7
    slab = sizes["lat"] * per
    waves = jnp.asarray(twiddles(nlon, slab * sizes["sub"], sizes["sub"]))
    table = lax.dynamic_index_in_dim(waves, lax.axis_index("sub"), 0, keepdims=False)
    held = pl.BlockSpec(memory_space=pl.ANY)
    vmem = pl.BlockSpec(memory_space=pltpu.VMEM)
    return pl.pallas_call(
        functools.partial(dft_kernel, sizes, step, ahead),
        in_specs=[vmem, vmem, held],
        out_specs=[vmem] * sizes["lat"],
        out_shape=[jax.ShapeDtypeStruct((lat_rows, per, 128), BF16)] * sizes["lat"],
        scratch_shapes=[
            pltpu.VMEM(field.shape, F32),
            pltpu.VMEM((nlon, 256), BF16),
            pltpu.SemaphoreType.DMA((lat_rows // step,)),
        ],
        compiler_params=pltpu.CompilerParams(vmem_limit_bytes=48 << 20),
        cost_estimate=pl.CostEstimate(
            flops=2 * lat_rows * chans * nlon * 256, bytes_accessed=field.size * 4, transcendentals=0
        ),
        name="dft",
    )(modes, table, field)


def pick_kernel(sizes, ownership_ref, table_ref, modes_ref, *refs):
    *outs, legendre_ref, owner_ref, arrived, known = refs
    per = sizes["per"]
    rows, slab, _ = legendre_ref.shape
    share = lax.axis_index("rep") * sizes["ch"] + lax.axis_index("ch")
    owners = pltpu.make_async_copy(ownership_ref, owner_ref, known)
    owners.start()
    values = pltpu.make_async_copy(table_ref.at[pl.ds(share * rows, rows)], legendre_ref, arrived)
    values.start()
    owners.wait()
    row = owned_row(owner_ref, sizes, range(sizes["lat"])) - lax.axis_index("sub") * slab
    modes_ref[...] = jnp.broadcast_to(row, modes_ref.shape)
    pick = choice(modes_ref, slab).T[per : sizes["lat"] * per].astype(BF16)
    values.wait()
    for t in range(rows):
        picked = jnp.dot(pick, legendre_ref[t], preferred_element_type=F32)
        for i, out_ref in enumerate(outs):
            out_ref[t] = picked[i * per : (i + 1) * per].astype(BF16)


def pick_rows(table, ownership, sizes, rows):
    _, slab, degrees = table.shape
    per, others = sizes["per"], sizes["lat"] - 1
    held = pl.BlockSpec(memory_space=pl.ANY)
    return pl.pallas_call(
        functools.partial(pick_kernel, sizes),
        grid=(1,),
        in_specs=[held, held],
        out_specs=[pl.BlockSpec((8, 128), lambda i: (0, 0))]
        + [pl.BlockSpec((rows, per, degrees), lambda i: (0, 0, 0))] * others,
        out_shape=[jax.ShapeDtypeStruct((8, 128), jnp.int32)]
        + [jax.ShapeDtypeStruct((rows, per, degrees), BF16)] * others,
        scratch_shapes=[
            pltpu.VMEM((rows, slab, degrees), BF16),
            pltpu.SMEM(ownership.shape, jnp.int32),
            pltpu.SemaphoreType.DMA,
            pltpu.SemaphoreType.DMA,
        ],
        compiler_params=pltpu.CompilerParams(vmem_limit_bytes=56 * 1000 * 1000),
        cost_estimate=pl.CostEstimate(
            flops=2 * rows * slab * degrees * per * others,
            bytes_accessed=rows * slab * degrees * 2,
            transcendentals=0,
        ),
        name="pick_rows",
    )(ownership, table)


def pack_kernel(*refs):
    *parts, out_ref = refs
    rows = parts[0].shape[0]
    for i, part in enumerate(parts):
        out_ref[i * rows : (i + 1) * rows] = part[...]


def pack(parts):
    rows, per, width = parts[0].shape
    return pl.pallas_call(
        pack_kernel,
        out_shape=jax.ShapeDtypeStruct((len(parts) * rows, per, width), BF16),
        compiler_params=pltpu.CompilerParams(vmem_limit_bytes=16 << 20),
        name="pack",
    )(*parts)


def by_mode(rows, per, out_ref, scratch):
    depth = out_ref.shape[1]
    for i in range(scratch.shape[0]):
        scratch[i, : depth * per, :] = rows[:, i * 128 : (i + 1) * 128]
    for k in range(per):
        for i in range(scratch.shape[0]):
            out_ref[k, :, i * 128 : (i + 1) * 128] = scratch[
                i, pl.ds(k, depth, stride=per), :
            ].astype(BF16)


def widened(rows, before, after):
    blank = jnp.zeros((after - before, rows.shape[1]), F32)
    parts = []
    for i in range(rows.shape[0] // before):
        parts += [rows[i * before : (i + 1) * before], blank]
    return jnp.concatenate(parts, axis=0)


def own_kernel(sizes, deep, modes_ref, legendre_ref, out_ref, picked, scratch):
    per = sizes["per"]
    lat_rows, slab, degrees = legendre_ref.shape
    share = lat_rows // (sizes["rep"] * sizes["ch"])
    pick = choice(modes_ref, slab).T[:per].astype(BF16)
    for t in range(lat_rows):
        picked[t * per : (t + 1) * per, :] = jnp.dot(pick, legendre_ref[t], preferred_element_type=F32)
    by_mode(widened(picked[...], share * per, deep * per), per, out_ref, scratch)


def own_table(by_latitude, modes, deep, sizes):
    lat_rows, _, degrees = by_latitude.shape
    per = sizes["per"]
    depth = sizes["rep"] * sizes["ch"] * deep
    vmem = pl.BlockSpec(memory_space=pltpu.VMEM)
    return pl.pallas_call(
        functools.partial(own_kernel, sizes, deep),
        in_specs=[vmem, vmem],
        out_specs=vmem,
        out_shape=jax.ShapeDtypeStruct((per, depth, degrees), BF16),
        scratch_shapes=[
            pltpu.VMEM((lat_rows * per, degrees), F32),
            pltpu.VMEM((degrees // 128, (depth + 1) * per, 128), F32),
        ],
        compiler_params=pltpu.CompilerParams(vmem_limit_bytes=32 << 20),
        cost_estimate=pl.CostEstimate(flops=3_000_000_000, bytes_accessed=1000, transcendentals=0),
        name="own_table",
    )(modes, by_latitude)


def turn_kernel(share, deep, rows_ref, out_ref, scratch):
    rows, per, width = rows_ref.shape
    values = rows_ref[...].astype(F32).reshape(rows * per, width)
    by_mode(widened(values, share * per, deep * per), per, out_ref, scratch)


def turn(rows, share, deep):
    total, per, degrees = rows.shape
    depth = total // share * deep
    return pl.pallas_call(
        functools.partial(turn_kernel, share, deep),
        out_shape=jax.ShapeDtypeStruct((per, depth, degrees), BF16),
        scratch_shapes=[pltpu.VMEM((degrees // 128, (depth + 1) * per, 128), F32)],
        compiler_params=pltpu.CompilerParams(vmem_limit_bytes=16 << 20),
        cost_estimate=pl.CostEstimate(flops=1000, bytes_accessed=1000, transcendentals=0),
        name="turn",
    )(rows)


def mix_kernel(sizes, shifts, deep, near_ref, far_ref, w_near, w_far, out_ref, scratch):
    rows, per, width = near_ref.shape
    plane = sizes["rep"] * sizes["ch"]
    lat_rows = rows // len(shifts)
    share = lat_rows // plane
    q = lax.axis_index("rep") * sizes["ch"] + lax.axis_index("ch")
    nt = (((1,), (1,)), ((), ()))
    w_both = jnp.concatenate([w_near[...], w_far[...]], axis=1)
    parts = []
    for i, shift in enumerate(shifts):
        for d in range(plane):
            at = d if shift == 0 else jnp.bitwise_xor(q, d)
            part = pl.ds(i * lat_rows + at * share, share)
            a = near_ref[part].reshape(share * per, width)
            b = far_ref[part].reshape(share * per, width)
            both = jnp.concatenate([a, b], axis=1)
            mixed = lax.dot_general(both, w_both, nt, preferred_element_type=F32)
            parts.append(widened(mixed, share * per, deep * per))
    by_mode(jnp.concatenate(parts, axis=0), per, out_ref, scratch)


def mix(near, far, w_near, w_far, shifts, deep, sizes):
    rows, per, width = near.shape
    depth = len(shifts) * sizes["rep"] * sizes["ch"] * deep
    return pl.pallas_call(
        functools.partial(mix_kernel, sizes, shifts, deep),
        out_shape=jax.ShapeDtypeStruct((per, depth, width), BF16),
        scratch_shapes=[pltpu.VMEM((1, (depth + 1) * per, width), F32)],
        compiler_params=pltpu.CompilerParams(vmem_limit_bytes=16 << 20),
        cost_estimate=pl.CostEstimate(
            flops=2 * 2 * near.size * width, bytes_accessed=near.size * 4, transcendentals=0
        ),
        name="mix",
    )(near, far, w_near, w_far)


def cross_kernel(near_ref, far_ref, w_near, w_far, *outs):
    rows, per, width = near_ref.shape
    lat_rows = rows // len(outs)
    nt = (((1,), (1,)), ((), ()))
    w_both = jnp.concatenate([w_near[...], w_far[...]], axis=1)
    for i, out_ref in enumerate(outs):
        part = slice(i * lat_rows, (i + 1) * lat_rows)
        a = near_ref[part].reshape(lat_rows * per, width)
        b = far_ref[part].reshape(lat_rows * per, width)
        both = jnp.concatenate([a, b], axis=1)
        mixed = lax.dot_general(both, w_both, nt, preferred_element_type=F32)
        out_ref[...] = mixed.astype(BF16).reshape(lat_rows, per, width)


def cross_parts(near, far, w_near, w_far, parts):
    rows, per, width = near.shape
    return pl.pallas_call(
        cross_kernel,
        out_shape=[jax.ShapeDtypeStruct((rows // parts, per, width), BF16)] * parts,
        compiler_params=pltpu.CompilerParams(vmem_limit_bytes=16 << 20),
        cost_estimate=pl.CostEstimate(flops=1000, bytes_accessed=1000, transcendentals=0),
        name="cross",
    )(near, far, w_near, w_far)


def arrange_kernel(sizes, shift, deep, rows_ref, out_ref, scratch):
    lat_rows, per, width = rows_ref.shape
    plane = sizes["rep"] * sizes["ch"]
    share = lat_rows // plane
    q = lax.axis_index("rep") * sizes["ch"] + lax.axis_index("ch")
    parts = []
    for d in range(plane):
        at = d if shift == 0 else jnp.bitwise_xor(q, d)
        part = rows_ref[pl.ds(at * share, share)].astype(F32).reshape(share * per, width)
        parts.append(widened(part, share * per, deep * per))
    by_mode(jnp.concatenate(parts, axis=0), per, out_ref, scratch)


def arrange(rows, shift, deep, sizes):
    _, per, width = rows.shape
    depth = sizes["rep"] * sizes["ch"] * deep
    return pl.pallas_call(
        functools.partial(arrange_kernel, sizes, shift, deep),
        out_shape=jax.ShapeDtypeStruct((per, depth, width), BF16),
        scratch_shapes=[pltpu.VMEM((1, (depth + 1) * per, width), F32)],
        compiler_params=pltpu.CompilerParams(vmem_limit_bytes=16 << 20),
        cost_estimate=pl.CostEstimate(flops=4_000_000_000, bytes_accessed=1000, transcendentals=0),
        name="arrange",
    )(rows)


def contract_kernel(order, plane, group, *refs):
    *spectra, own = refs[: -plane - 3]
    *tables, out_ref, mixed, left = refs[-plane - 3 :]
    deep = own.shape[1] // plane
    _, per, half, _ = mixed.shape

    def part_copy(i):
        part = pl.ds(i * group, group)
        return pltpu.make_async_copy(mixed.at[:, part], out_ref.at[:, part], left.at[i])

    @pl.loop(0, per // group, unroll=True)
    def _(i):
        for j in range(group):
            k = i * group + j
            a = jnp.concatenate([part[k] for part in spectra], axis=0)
            pieces = [own[k]]
            for s in order:
                pieces += [table[k, (s - 1) * deep : s * deep] for table in tables]
            b = jnp.concatenate(pieces, axis=0)
            c = lax.dot_general(a, b, (((0,), (0,)), ((), ())), preferred_element_type=F32)
            mixed[0, k] = c[:half].astype(BF16)
            mixed[1, k] = c[half:].astype(BF16)
        part_copy(i).start()

    @pl.loop(0, per // group)
    def _(i):
        part_copy(i).wait()


def contract(spectra, own, tables, order):
    per, _, width = spectra[0].shape
    degrees = own.shape[2]
    group = 6
    vmem = pl.BlockSpec(memory_space=pltpu.VMEM)
    shape = (2, per, width // 2, degrees)
    return pl.pallas_call(
        functools.partial(contract_kernel, order, len(tables), group),
        in_specs=[vmem] * (len(spectra) + 1 + len(tables)),
        out_specs=pl.BlockSpec(memory_space=pl.ANY),
        out_shape=jax.ShapeDtypeStruct(shape, BF16),
        scratch_shapes=[pltpu.VMEM(shape, BF16), pltpu.SemaphoreType.DMA((per // group,))],
        compiler_params=pltpu.CompilerParams(vmem_limit_bytes=40 << 20),
        name="contract",
    )(*spectra, own, *tables)


def mixing_weights(w_real, w_imag):
    half = w_real.shape[0]
    x = lax.axis_index("ch")
    out = []
    for side in (x, 1 - x):
        wr = lax.dynamic_slice_in_dim(w_real, side * half, half, 1)
        wi = lax.dynamic_slice_in_dim(w_imag, side * half, half, 1)
        out.append(
            jnp.concatenate(
                [jnp.concatenate([wr, -wi], axis=1), jnp.concatenate([wi, wr], axis=1)], axis=0
            )
        )
    return out


def fast(field, legendre, ownership, w_real, w_imag, sizes):
    lats, plane = sizes["lat"], sizes["rep"] * sizes["ch"]
    lat_rows = field.shape[0]
    share, deep = lat_rows // plane, (lat_rows // plane + 7) // 8 * 8
    by_latitude = jnp.transpose(legendre, (1, 0, 2))
    forward = lambda v, s: lax.ppermute(v, "lat", [(i, (i + s) % lats) for i in range(lats)])
    across = lambda v: lax.ppermute(v, "ch", [(0, 1), (1, 0)])
    beyond = lambda v: lax.ppermute(v, "rep", [(0, 1), (1, 0)])
    after = lambda v, *before: lax.optimization_barrier((v, *before))[0]
    modes, *sent = pick_rows(by_latitude, ownership, sizes, share)
    landed = [forward(v, s) for s, v in enumerate(sent, 1)]
    spectra = dft(field, modes, sizes)
    w_near, w_far = mixing_weights(w_real, w_imag)
    mine = pack(landed)
    beside = across(mine)
    beyond_mine = beyond(mine)
    early = pack([spectra[0], spectra[2]])
    far_early = across(early)
    own = own_table(by_latitude, after(modes, far_early), deep, sizes)
    near3 = forward(after(spectra[3], mine), 3)
    near1 = forward(after(spectra[1], mine), 1)
    zero, *sums = cross_parts(early, far_early, w_near, w_far, 2)
    mixed = [arrange(zero, 0, deep, sizes)]
    sum2 = forward(sums[0], 2)
    late0 = near3
    late1 = near1
    beyond_beside = beyond(beside)
    far_late0 = across(late0)
    far_late1 = across(late1)
    far_late1 = after(far_late1, sum2)
    tables = [turn(v, share, deep) for v in (mine, beside, beyond_mine, beyond_beside)]
    mixed.append(mix(late0, far_late0, w_near, w_far, (3,), deep, sizes))
    mixed.append(mix(late1, far_late1, w_near, w_far, (1,), deep, sizes))
    mixed += [arrange(v, s, deep, sizes) for v, s in ((sum2, 2),)]
    return contract(mixed, own, tables, (3, 1, 2))


def fourier_rows(flat_field, modes, lat_rows, chans, nlon):
    longitude = jnp.arange(nlon, dtype=jnp.int32)
    phase = longitude[:, None] * modes[None, :] % nlon
    angle = phase.astype(jnp.float32) * (2.0 * math.pi / nlon)
    scale = 1.0 / math.sqrt(nlon)
    real_part = (
        jnp.dot(
            flat_field,
            jnp.cos(angle),
            precision=lax.Precision.HIGHEST,
            preferred_element_type=jnp.float32,
        )
        * scale
    )
    imag_part = (
        -jnp.dot(
            flat_field,
            jnp.sin(angle),
            precision=lax.Precision.HIGHEST,
            preferred_element_type=jnp.float32,
        )
        * scale
    )
    both = jnp.stack([real_part, imag_part]).reshape(2, lat_rows, chans, modes.shape[0])
    both = jnp.transpose(both, (3, 1, 0, 2)).reshape(modes.shape[0], lat_rows, 2 * chans)
    return both.astype(jnp.bfloat16)


def general(field, legendre, ownership, w_real, w_imag):
    lat_rows, chans, nlon = field.shape
    degrees = legendre.shape[2]
    slab_modes = legendre.shape[0]
    blocks = lax.axis_size("lat")
    halves = lax.axis_size("sub")
    per_block = ownership.shape[0] // (blocks * halves)
    my_modes = lax.dynamic_index_in_dim(
        ownership.reshape(blocks, halves, per_block), lax.axis_index("sub"), 1, keepdims=False
    ).reshape(blocks * per_block)
    slab_index = my_modes - lax.axis_index("sub") * slab_modes
    flat_field = field.reshape(lat_rows * chans, nlon)
    spectra_rows = fourier_rows(flat_field, my_modes, lat_rows, chans, nlon)
    table_rows = jnp.take(legendre, slab_index, axis=0)
    spectra_all, tables_all = (
        lax.all_to_all(spectra_rows, "lat", split_axis=0, concat_axis=1, tiled=True),
        lax.all_to_all(table_rows, "lat", split_axis=0, concat_axis=1, tiled=True),
    )
    spectra_all = spectra_all.reshape(per_block, blocks, lat_rows, 2 * chans)
    tables_all = tables_all.reshape(per_block, blocks, lat_rows, degrees)
    block_part = jnp.einsum(
        "kbtc,kbtl->kbcl", spectra_all, tables_all, preferred_element_type=jnp.float32
    )
    total = jnp.sum(block_part, axis=1)
    coeff = total.astype(jnp.bfloat16).reshape(per_block, 2, chans, degrees)
    piece = lax.all_gather(coeff, "ch", axis=2, tiled=True)
    real_in = piece[:, 0]
    imag_in = piece[:, 1]
    real_out = jnp.einsum(
        "oc,kcl->kol", w_real, real_in, preferred_element_type=jnp.float32
    ) - jnp.einsum("oc,kcl->kol", w_imag, imag_in, preferred_element_type=jnp.float32)
    imag_out = jnp.einsum(
        "oc,kcl->kol", w_real, imag_in, preferred_element_type=jnp.float32
    ) + jnp.einsum("oc,kcl->kol", w_imag, real_in, preferred_element_type=jnp.float32)
    mixed = jnp.stack([real_out, imag_out])
    return mixed.astype(jnp.bfloat16)


def per_device(sizes, field, legendre, ownership, w_real, w_imag):
    lat_rows, chans, nlon = field.shape
    sizes = dict(sizes, per=ownership.shape[0] // (sizes["lat"] * sizes["sub"]))
    plane = sizes["rep"] * sizes["ch"]
    fits = (
        sizes["ch"] == 2
        and sizes["rep"] == 2
        and sizes["lat"] == 4
        and 2 * chans == 128
        and lat_rows % plane == 0
        and lat_rows % 28 == 0
        and sizes["per"] % 8 == 0
        and sizes["lat"] * sizes["per"] <= 128
        and legendre.shape[2] % 128 == 0
    )
    if fits:
        return fast(field, legendre, ownership, w_real, w_imag, sizes)
    return general(field, legendre, ownership, w_real, w_imag)


def solution(mesh):
    in_specs = (
        P(("rep", "lat"), "ch", None),
        P("sub", "lat", None),
        P(),
        P("ch", None),
        P("ch", None),
    )
    out_specs = P("rep", ("lat", "sub"), "ch", None)
    return jax.shard_map(
        functools.partial(per_device, dict(mesh.shape)),
        mesh=mesh,
        in_specs=in_specs,
        out_specs=out_specs,
        check_vma=False,
    )
```

```python
import functools
import math

import jax
import jax.numpy as jnp
import numpy as np
from jax import lax
from jax.experimental import pallas as pl
from jax.experimental.pallas import tpu as pltpu
from jax.sharding import PartitionSpec as P

F32 = jnp.float32
BF16 = jnp.bfloat16


def twiddles(nlon, modes, parts):
    phase = np.arange(nlon)[:, None] * np.arange(modes)[None, :] % nlon
    angle = phase * (2.0 * math.pi / nlon)
    scale = 1.0 / math.sqrt(nlon)
    waves = np.stack([np.cos(angle) * scale, -np.sin(angle) * scale]).astype(BF16)
    return np.moveaxis(waves.reshape(2, nlon, parts, modes // parts), 2, 0).copy()


def position(shift, k, sizes):
    owner = lax.rem(lax.axis_index("lat") + shift, sizes["lat"])
    return (owner * sizes["sub"] + lax.axis_index("sub")) * sizes["per"] + k


def owned_row(owner_ref, sizes, shifts):
    lane = lax.broadcasted_iota(jnp.int32, (1, 128), 1)
    row = jnp.full((1, 128), -1, jnp.int32)
    j = 0
    for shift in shifts:
        base = position(shift, 0, sizes)
        for k in range(sizes["per"]):
            row = jnp.where(lane == j, owner_ref[base + k], row)
            j += 1
    return row


def choice(modes_ref, slab):
    row = lax.broadcasted_iota(jnp.int32, (slab, 128), 0)
    return (row == modes_ref[:1]).astype(F32)


def dft_kernel(sizes, step, ahead, modes_ref, table_ref, field_ref, *refs):
    *outs, grid_values, chosen, arrived = refs
    per = sizes["per"]
    rows, chans, nlon = grid_values.shape
    steps = rows // step

    def part_copy(i):
        part = pl.ds(i * step, step)
        return pltpu.make_async_copy(field_ref.at[part], grid_values.at[part], arrived.at[i])

    for i in range(ahead):
        part_copy(i).start()

    pick = choice(modes_ref, table_ref.shape[2]).astype(BF16)
    for r in range(2):
        chosen[:, r * 128 : (r + 1) * 128] = jnp.dot(
            table_ref[r], pick, preferred_element_type=F32
        ).astype(BF16)

    @pl.loop(0, steps)
    def _(i):
        part_copy(i).wait()

        @pl.when(i + ahead < steps)
        def _():
            part_copy(i + ahead).start()

        values = grid_values[pl.ds(i * step, step)].reshape(step * chans, nlon).astype(BF16)
        spectrum = jnp.dot(values, chosen[...], preferred_element_type=F32)
        for t in range(step):
            part = spectrum[t * chans : (t + 1) * chans]
            turned = jnp.concatenate([part[:, :128], part[:, 128:]], axis=0).T
            for shift in range(sizes["lat"]):
                outs[shift][i * step + t] = turned[shift * per : (shift + 1) * per].astype(BF16)


def dft(field, modes, sizes):
    lat_rows, chans, nlon = field.shape
    per, step, ahead = sizes["per"], 4, 7
    slab = sizes["lat"] * per
    waves = jnp.asarray(twiddles(nlon, slab * sizes["sub"], sizes["sub"]))
    table = lax.dynamic_index_in_dim(waves, lax.axis_index("sub"), 0, keepdims=False)
    held = pl.BlockSpec(memory_space=pl.ANY)
    vmem = pl.BlockSpec(memory_space=pltpu.VMEM)
    return pl.pallas_call(
        functools.partial(dft_kernel, sizes, step, ahead),
        in_specs=[vmem, vmem, held],
        out_specs=[vmem] * sizes["lat"],
        out_shape=[jax.ShapeDtypeStruct((lat_rows, per, 128), BF16)] * sizes["lat"],
        scratch_shapes=[
            pltpu.VMEM(field.shape, F32),
            pltpu.VMEM((nlon, 256), BF16),
            pltpu.SemaphoreType.DMA((lat_rows // step,)),
        ],
        compiler_params=pltpu.CompilerParams(vmem_limit_bytes=48 << 20),
        cost_estimate=pl.CostEstimate(
            flops=2 * lat_rows * chans * nlon * 256, bytes_accessed=field.size * 4, transcendentals=0
        ),
        name="dft",
    )(modes, table, field)


def pick_kernel(sizes, ownership_ref, table_ref, modes_ref, *refs):
    *outs, legendre_ref, owner_ref, arrived, known = refs
    per = sizes["per"]
    rows, slab, _ = legendre_ref.shape
    share = lax.axis_index("rep") * sizes["ch"] + lax.axis_index("ch")
    owners = pltpu.make_async_copy(ownership_ref, owner_ref, known)
    owners.start()
    values = pltpu.make_async_copy(table_ref.at[pl.ds(share * rows, rows)], legendre_ref, arrived)
    values.start()
    owners.wait()
    row = owned_row(owner_ref, sizes, range(sizes["lat"])) - lax.axis_index("sub") * slab
    modes_ref[...] = jnp.broadcast_to(row, modes_ref.shape)
    pick = choice(modes_ref, slab).T[per : sizes["lat"] * per].astype(BF16)
    values.wait()
    for t in range(rows):
        picked = jnp.dot(pick, legendre_ref[t], preferred_element_type=F32)
        for i, out_ref in enumerate(outs):
            out_ref[t] = picked[i * per : (i + 1) * per].astype(BF16)


def pick_rows(table, ownership, sizes, rows):
    _, slab, degrees = table.shape
    per, others = sizes["per"], sizes["lat"] - 1
    held = pl.BlockSpec(memory_space=pl.ANY)
    return pl.pallas_call(
        functools.partial(pick_kernel, sizes),
        grid=(1,),
        in_specs=[held, held],
        out_specs=[pl.BlockSpec((8, 128), lambda i: (0, 0))]
        + [pl.BlockSpec((rows, per, degrees), lambda i: (0, 0, 0))] * others,
        out_shape=[jax.ShapeDtypeStruct((8, 128), jnp.int32)]
        + [jax.ShapeDtypeStruct((rows, per, degrees), BF16)] * others,
        scratch_shapes=[
            pltpu.VMEM((rows, slab, degrees), BF16),
            pltpu.SMEM(ownership.shape, jnp.int32),
            pltpu.SemaphoreType.DMA,
            pltpu.SemaphoreType.DMA,
        ],
        compiler_params=pltpu.CompilerParams(vmem_limit_bytes=56 * 1000 * 1000),
        cost_estimate=pl.CostEstimate(
            flops=2 * rows * slab * degrees * per * others,
            bytes_accessed=rows * slab * degrees * 2,
            transcendentals=0,
        ),
        name="pick_rows",
    )(ownership, table)


def pack_kernel(*refs):
    *parts, out_ref = refs
    rows = parts[0].shape[0]
    for i, part in enumerate(parts):
        out_ref[i * rows : (i + 1) * rows] = part[...]


def pack(parts):
    rows, per, width = parts[0].shape
    return pl.pallas_call(
        pack_kernel,
        out_shape=jax.ShapeDtypeStruct((len(parts) * rows, per, width), BF16),
        compiler_params=pltpu.CompilerParams(vmem_limit_bytes=16 << 20),
        name="pack",
    )(*parts)


def by_mode(rows, per, out_ref, scratch):
    depth = out_ref.shape[1]
    for i in range(scratch.shape[0]):
        scratch[i, : depth * per, :] = rows[:, i * 128 : (i + 1) * 128]
    for k in range(per):
        for i in range(scratch.shape[0]):
            out_ref[k, :, i * 128 : (i + 1) * 128] = scratch[
                i, pl.ds(k, depth, stride=per), :
            ].astype(BF16)


def widened(rows, before, after):
    blank = jnp.zeros((after - before, rows.shape[1]), F32)
    parts = []
    for i in range(rows.shape[0] // before):
        parts += [rows[i * before : (i + 1) * before], blank]
    return jnp.concatenate(parts, axis=0)


def own_kernel(sizes, deep, modes_ref, legendre_ref, out_ref, picked, scratch):
    per = sizes["per"]
    lat_rows, slab, degrees = legendre_ref.shape
    share = lat_rows // (sizes["rep"] * sizes["ch"])
    pick = choice(modes_ref, slab).T[:per].astype(BF16)
    for t in range(lat_rows):
        picked[t * per : (t + 1) * per, :] = jnp.dot(pick, legendre_ref[t], preferred_element_type=F32)
    by_mode(widened(picked[...], share * per, deep * per), per, out_ref, scratch)


def own_table(by_latitude, modes, deep, sizes):
    lat_rows, _, degrees = by_latitude.shape
    per = sizes["per"]
    depth = sizes["rep"] * sizes["ch"] * deep
    vmem = pl.BlockSpec(memory_space=pltpu.VMEM)
    return pl.pallas_call(
        functools.partial(own_kernel, sizes, deep),
        in_specs=[vmem, vmem],
        out_specs=vmem,
        out_shape=jax.ShapeDtypeStruct((per, depth, degrees), BF16),
        scratch_shapes=[
            pltpu.VMEM((lat_rows * per, degrees), F32),
            pltpu.VMEM((degrees // 128, (depth + 1) * per, 128), F32),
        ],
        compiler_params=pltpu.CompilerParams(vmem_limit_bytes=32 << 20),
        cost_estimate=pl.CostEstimate(flops=3_000_000_000, bytes_accessed=1000, transcendentals=0),
        name="own_table",
    )(modes, by_latitude)


def turn_kernel(share, deep, rows_ref, out_ref, scratch):
    rows, per, width = rows_ref.shape
    values = rows_ref[...].astype(F32).reshape(rows * per, width)
    by_mode(widened(values, share * per, deep * per), per, out_ref, scratch)


def turn(rows, share, deep):
    total, per, degrees = rows.shape
    depth = total // share * deep
    return pl.pallas_call(
        functools.partial(turn_kernel, share, deep),
        out_shape=jax.ShapeDtypeStruct((per, depth, degrees), BF16),
        scratch_shapes=[pltpu.VMEM((degrees // 128, (depth + 1) * per, 128), F32)],
        compiler_params=pltpu.CompilerParams(vmem_limit_bytes=16 << 20),
        cost_estimate=pl.CostEstimate(flops=1000, bytes_accessed=1000, transcendentals=0),
        name="turn",
    )(rows)


def mix_kernel(sizes, shifts, deep, near_ref, far_ref, weights, out_ref, scratch):
    rows, per, width = near_ref.shape
    plane = sizes["rep"] * sizes["ch"]
    lat_rows = rows // len(shifts)
    share = lat_rows // plane
    q = lax.axis_index("rep") * sizes["ch"] + lax.axis_index("ch")
    nt = (((1,), (1,)), ((), ()))
    w_both = weights[...]
    parts = []
    for i, shift in enumerate(shifts):
        for d in range(plane):
            at = d if shift == 0 else jnp.bitwise_xor(q, d)
            part = pl.ds(i * lat_rows + at * share, share)
            a = near_ref[part].reshape(share * per, width)
            b = far_ref[part].reshape(share * per, width)
            both = jnp.concatenate([a, b], axis=1)
            mixed = lax.dot_general(both, w_both, nt, preferred_element_type=F32)
            parts.append(widened(mixed, share * per, deep * per))
    by_mode(jnp.concatenate(parts, axis=0), per, out_ref, scratch)


def mix(near, far, weights, shifts, deep, sizes):
    rows, per, width = near.shape
    depth = len(shifts) * sizes["rep"] * sizes["ch"] * deep
    return pl.pallas_call(
        functools.partial(mix_kernel, sizes, shifts, deep),
        out_shape=jax.ShapeDtypeStruct((per, depth, width), BF16),
        scratch_shapes=[pltpu.VMEM((1, (depth + 1) * per, width), F32)],
        compiler_params=pltpu.CompilerParams(vmem_limit_bytes=16 << 20),
        cost_estimate=pl.CostEstimate(
            flops=2 * 2 * near.size * width, bytes_accessed=near.size * 4, transcendentals=0
        ),
        name="mix",
    )(near, far, weights)


def cross_kernel(near_ref, far_ref, weights, *outs):
    rows, per, width = near_ref.shape
    lat_rows = rows // len(outs)
    nt = (((1,), (1,)), ((), ()))
    w_both = weights[...]
    for i, out_ref in enumerate(outs):
        part = slice(i * lat_rows, (i + 1) * lat_rows)
        a = near_ref[part].reshape(lat_rows * per, width)
        b = far_ref[part].reshape(lat_rows * per, width)
        both = jnp.concatenate([a, b], axis=1)
        mixed = lax.dot_general(both, w_both, nt, preferred_element_type=F32)
        out_ref[...] = mixed.astype(BF16).reshape(lat_rows, per, width)


def cross_parts(near, far, weights, parts):
    rows, per, width = near.shape
    return pl.pallas_call(
        cross_kernel,
        out_shape=[jax.ShapeDtypeStruct((rows // parts, per, width), BF16)] * parts,
        compiler_params=pltpu.CompilerParams(vmem_limit_bytes=16 << 20),
        cost_estimate=pl.CostEstimate(flops=1000, bytes_accessed=1000, transcendentals=0),
        name="cross",
    )(near, far, weights)


def arrange_kernel(sizes, shift, deep, rows_ref, out_ref, scratch):
    lat_rows, per, width = rows_ref.shape
    plane = sizes["rep"] * sizes["ch"]
    share = lat_rows // plane
    q = lax.axis_index("rep") * sizes["ch"] + lax.axis_index("ch")
    parts = []
    for d in range(plane):
        at = d if shift == 0 else jnp.bitwise_xor(q, d)
        part = rows_ref[pl.ds(at * share, share)].astype(F32).reshape(share * per, width)
        parts.append(widened(part, share * per, deep * per))
    by_mode(jnp.concatenate(parts, axis=0), per, out_ref, scratch)


def arrange(rows, shift, deep, sizes):
    _, per, width = rows.shape
    depth = sizes["rep"] * sizes["ch"] * deep
    return pl.pallas_call(
        functools.partial(arrange_kernel, sizes, shift, deep),
        out_shape=jax.ShapeDtypeStruct((per, depth, width), BF16),
        scratch_shapes=[pltpu.VMEM((1, (depth + 1) * per, width), F32)],
        compiler_params=pltpu.CompilerParams(vmem_limit_bytes=16 << 20),
        cost_estimate=pl.CostEstimate(flops=4_000_000_000, bytes_accessed=1000, transcendentals=0),
        name="arrange",
    )(rows)


def contract_kernel(order, plane, group, *refs):
    *spectra, own = refs[: -plane - 3]
    *tables, out_ref, mixed, left = refs[-plane - 3 :]
    deep = own.shape[1] // plane
    _, per, half, _ = mixed.shape

    def part_copy(i):
        part = pl.ds(i * group, group)
        return pltpu.make_async_copy(mixed.at[:, part], out_ref.at[:, part], left.at[i])

    @pl.loop(0, per // group, unroll=True)
    def _(i):
        for j in range(group):
            k = i * group + j
            a = jnp.concatenate([part[k] for part in spectra], axis=0)
            pieces = [own[k]]
            for s in order:
                pieces += [table[k, (s - 1) * deep : s * deep] for table in tables]
            b = jnp.concatenate(pieces, axis=0)
            c = lax.dot_general(a, b, (((0,), (0,)), ((), ())), preferred_element_type=F32)
            mixed[0, k] = c[:half].astype(BF16)
            mixed[1, k] = c[half:].astype(BF16)
        part_copy(i).start()

    @pl.loop(0, per // group)
    def _(i):
        part_copy(i).wait()


def contract(spectra, own, tables, order):
    per, _, width = spectra[0].shape
    degrees = own.shape[2]
    group = 6
    vmem = pl.BlockSpec(memory_space=pltpu.VMEM)
    shape = (2, per, width // 2, degrees)
    return pl.pallas_call(
        functools.partial(contract_kernel, order, len(tables), group),
        in_specs=[vmem] * (len(spectra) + 1 + len(tables)),
        out_specs=pl.BlockSpec(memory_space=pl.ANY),
        out_shape=jax.ShapeDtypeStruct(shape, BF16),
        scratch_shapes=[pltpu.VMEM(shape, BF16), pltpu.SemaphoreType.DMA((per // group,))],
        compiler_params=pltpu.CompilerParams(vmem_limit_bytes=40 << 20),
        name="contract",
    )(*spectra, own, *tables)


def mixing_weights(w_real, w_imag):
    half = w_real.shape[0]
    first = lax.axis_index("ch") == 0
    columns = [[], []]
    sides = []
    for w in (w_real.astype(F32), w_imag.astype(F32)):
        low, high = w[:, :half], w[:, half:]
        sides.append((jnp.where(first, low, high), jnp.where(first, high, low)))
    for side in range(2):
        real, imag = sides[0][side], sides[1][side]
        columns[0] += [real, -imag]
        columns[1] += [imag, real]
    return jnp.concatenate([jnp.concatenate(row, axis=1) for row in columns], axis=0)


def weigh_kernel(w_real, w_imag, out_ref):
    out_ref[...] = mixing_weights(w_real[...], w_imag[...]).astype(BF16)


def weigh(w_real, w_imag):
    half, chans = w_real.shape
    return pl.pallas_call(
        weigh_kernel,
        out_shape=jax.ShapeDtypeStruct((2 * half, 2 * chans), BF16),
        compiler_params=pltpu.CompilerParams(vmem_limit_bytes=16 << 20),
        cost_estimate=pl.CostEstimate(flops=3_000_000_000, bytes_accessed=1000, transcendentals=0),
        name="weigh",
    )(w_real, w_imag)


def fast(field, legendre, ownership, w_real, w_imag, sizes):
    lats, plane = sizes["lat"], sizes["rep"] * sizes["ch"]
    lat_rows = field.shape[0]
    share, deep = lat_rows // plane, (lat_rows // plane + 7) // 8 * 8
    by_latitude = jnp.transpose(legendre, (1, 0, 2))
    forward = lambda v, s: lax.ppermute(v, "lat", [(i, (i + s) % lats) for i in range(lats)])
    across = lambda v: lax.ppermute(v, "ch", [(0, 1), (1, 0)])
    beyond = lambda v: lax.ppermute(v, "rep", [(0, 1), (1, 0)])
    after = lambda v, *before: lax.optimization_barrier((v, *before))[0]
    modes, *sent = pick_rows(by_latitude, ownership, sizes, share)
    landed = [forward(v, s) for s, v in enumerate(sent, 1)]
    spectra = dft(field, modes, sizes)
    weights = weigh(w_real, w_imag)
    mine = pack(landed)
    beside = across(mine)
    beyond_mine = beyond(mine)
    early = pack([spectra[0], spectra[2]])
    far_early = across(early)
    own = own_table(by_latitude, after(modes, far_early), deep, sizes)
    near3 = forward(after(spectra[3], mine), 3)
    near1 = forward(after(spectra[1], mine), 1)
    zero, *sums = cross_parts(early, far_early, weights, 2)
    mixed = [arrange(zero, 0, deep, sizes)]
    sum2 = forward(sums[0], 2)
    late0 = near3
    late1 = near1
    beyond_beside = beyond(beside)
    far_late0 = across(late0)
    far_late1 = across(late1)
    far_late1 = after(far_late1, sum2)
    tables = [turn(v, share, deep) for v in (mine, beside, beyond_mine, beyond_beside)]
    mixed.append(mix(late0, far_late0, weights, (3,), deep, sizes))
    mixed.append(mix(late1, far_late1, weights, (1,), deep, sizes))
    mixed += [arrange(v, s, deep, sizes) for v, s in ((sum2, 2),)]
    return contract(mixed, own, tables, (3, 1, 2))


def fourier_rows(flat_field, modes, lat_rows, chans, nlon):
    longitude = jnp.arange(nlon, dtype=jnp.int32)
    phase = longitude[:, None] * modes[None, :] % nlon
    angle = phase.astype(jnp.float32) * (2.0 * math.pi / nlon)
    scale = 1.0 / math.sqrt(nlon)
    real_part = (
        jnp.dot(
            flat_field,
            jnp.cos(angle),
            precision=lax.Precision.HIGHEST,
            preferred_element_type=jnp.float32,
        )
        * scale
    )
    imag_part = (
        -jnp.dot(
            flat_field,
            jnp.sin(angle),
            precision=lax.Precision.HIGHEST,
            preferred_element_type=jnp.float32,
        )
        * scale
    )
    both = jnp.stack([real_part, imag_part]).reshape(2, lat_rows, chans, modes.shape[0])
    both = jnp.transpose(both, (3, 1, 0, 2)).reshape(modes.shape[0], lat_rows, 2 * chans)
    return both.astype(jnp.bfloat16)


def general(field, legendre, ownership, w_real, w_imag):
    lat_rows, chans, nlon = field.shape
    degrees = legendre.shape[2]
    slab_modes = legendre.shape[0]
    blocks = lax.axis_size("lat")
    halves = lax.axis_size("sub")
    per_block = ownership.shape[0] // (blocks * halves)
    my_modes = lax.dynamic_index_in_dim(
        ownership.reshape(blocks, halves, per_block), lax.axis_index("sub"), 1, keepdims=False
    ).reshape(blocks * per_block)
    slab_index = my_modes - lax.axis_index("sub") * slab_modes
    flat_field = field.reshape(lat_rows * chans, nlon)
    spectra_rows = fourier_rows(flat_field, my_modes, lat_rows, chans, nlon)
    table_rows = jnp.take(legendre, slab_index, axis=0)
    spectra_all, tables_all = (
        lax.all_to_all(spectra_rows, "lat", split_axis=0, concat_axis=1, tiled=True),
        lax.all_to_all(table_rows, "lat", split_axis=0, concat_axis=1, tiled=True),
    )
    spectra_all = spectra_all.reshape(per_block, blocks, lat_rows, 2 * chans)
    tables_all = tables_all.reshape(per_block, blocks, lat_rows, degrees)
    block_part = jnp.einsum(
        "kbtc,kbtl->kbcl", spectra_all, tables_all, preferred_element_type=jnp.float32
    )
    total = jnp.sum(block_part, axis=1)
    coeff = total.astype(jnp.bfloat16).reshape(per_block, 2, chans, degrees)
    piece = lax.all_gather(coeff, "ch", axis=2, tiled=True)
    real_in = piece[:, 0]
    imag_in = piece[:, 1]
    real_out = jnp.einsum(
        "oc,kcl->kol", w_real, real_in, preferred_element_type=jnp.float32
    ) - jnp.einsum("oc,kcl->kol", w_imag, imag_in, preferred_element_type=jnp.float32)
    imag_out = jnp.einsum(
        "oc,kcl->kol", w_real, imag_in, preferred_element_type=jnp.float32
    ) + jnp.einsum("oc,kcl->kol", w_imag, real_in, preferred_element_type=jnp.float32)
    mixed = jnp.stack([real_out, imag_out])
    return mixed.astype(jnp.bfloat16)


def per_device(sizes, field, legendre, ownership, w_real, w_imag):
    lat_rows, chans, nlon = field.shape
    sizes = dict(sizes, per=ownership.shape[0] // (sizes["lat"] * sizes["sub"]))
    plane = sizes["rep"] * sizes["ch"]
    fits = (
        sizes["ch"] == 2
        and sizes["rep"] == 2
        and sizes["lat"] == 4
        and 2 * chans == 128
        and lat_rows % plane == 0
        and lat_rows % 28 == 0
        and sizes["per"] % 8 == 0
        and sizes["lat"] * sizes["per"] <= 128
        and legendre.shape[2] % 128 == 0
    )
    if fits:
        return fast(field, legendre, ownership, w_real, w_imag, sizes)
    return general(field, legendre, ownership, w_real, w_imag)


def solution(mesh):
    in_specs = (
        P(("rep", "lat"), "ch", None),
        P("sub", "lat", None),
        P(),
        P("ch", None),
        P("ch", None),
    )
    out_specs = P("rep", ("lat", "sub"), "ch", None)
    return jax.shard_map(
        functools.partial(per_device, dict(mesh.shape)),
        mesh=mesh,
        in_specs=in_specs,
        out_specs=out_specs,
        check_vma=False,
    )
```
